32 devices in a mesh: gx: 8 (over z, y), gy: 4 (over x, core).
Axes of the slice: x: 2, y: 2, z: 4, core: 2. Of those that a mesh axis runs over, the one named last changes fastest.
Arguments:
- water_content: float32 [16, 512, 2048], P(None, 'gx', 'gy'), may hold values from 0.15 to 0.35
- porosity: float32 [512, 2048], P('gx', 'gy'), may hold values from 0.4 to 0.5
- conduct: float32 [512, 2048], P('gx', 'gy'), may hold values from 0.05 to 0.5
- exponent: float32 [512, 2048], P('gx', 'gy'), may hold values from 3 to 6
- infiltration: float32 [512, 2048], P('gx', 'gy'), may hold values from 0.02 to 0.2
- column_target: int32 [512, 2048], P('gx', 'gy'), may hold values from 0 to 16383, as said below
- send_blocks: int32 [32, 32, 4], P(('gx', 'gy')), may hold values from -1 to 7, as said below
- prior_heads: float32 [256, 128], P(('gx', 'gy')), may hold values from -6 to 6
- block_pattern: int32 [256, 7], P(('gx', 'gy')), may hold values from -1 to 255, as said below
- aquifer_blocks: float32 [256, 7, 128, 128], P(('gx', 'gy')), as said below
Outputs:
- soil_water: float32 [16, 512, 2048], P(None, 'gx', 'gy')
- aquifer_heads: float32 [256, 128], P(('gx', 'gy'))
- column_heads: float32 [512, 2048], P('gx', 'gy')
The draws below stay inside these ranges and needn't reach their ends.
Inputs may be any that keep to these rules, and one draw needn't show every extreme that they name: send_blocks[d, o, s] is a block number of owner o or -1; the blocks of one (d, o) are distinct and the -1 entries come last; entries other than -1 stand only where o is d or the device next to d along gx or along gy, without wrap; send_blocks[d, d] holds 4 blocks, every neighbour at least one, and in every draw some owner receives 4 blocks from each of its neighbours. `column_target`: every column of device d's tile names an owner o that is d or next to d along gx or gy, a slot s with send_blocks[d, o, s] >= 0, and a cell below 128. block_pattern[r, 0] = r; every other entry is -1 or a block on r's own device or on the device next to it along gx or along gy, without wrap; no row names a block twice, and block s appears in row r exactly when r appears in row s. `aquifer_blocks`: blocks where block_pattern is -1 are zero; the block that row r holds for s is the transpose of the one that row s holds for r, and the assembled matrix is symmetric and strictly diagonally dominant with a positive diagonal.
All inputs are finite; a program needn't handle non-finite values.
Results may differ from the reference program's by a relative error of at most 0.0003.
Values sent between devices are 32-bit elements; how exact they have to be, the bound alone decides.
No kernel may reach another device: no remote copies, remote signals or barrier semaphores. Data moves between devices by JAX's collectives and lax.ppermute only.
A program may use at most 64 MiB of HBM per device.

```python
import math
import jax
import jax.numpy as jnp
from jax import lax

NL = 16
SX = 64
SY = 512
AB_DEV = 8
SLOTS = 4
BS = 128
SWEEPS = 8
ITERS = 3
NSX = 512
NSY = 2048
NBLK = 256
N_GY = 4
DEVICES = 32


def routing_of(key):
    gy_count = NSY // SY
    device = jnp.arange(DEVICES, dtype=jnp.int32)[:, None]
    owners = jnp.arange(DEVICES, dtype=jnp.int32)[None, :]
    dev_x = device // gy_count
    dev_y = device % gy_count
    own_x = owners // gy_count
    own_y = owners % gy_count
    beside = (jnp.abs(dev_x - own_x) == 1) & (dev_y == own_y) | (jnp.abs(dev_y - own_y) == 1) & (dev_x == own_x)
    counts = jax.random.randint(jax.random.fold_in(key, 11), (DEVICES, DEVICES), 1, SLOTS + 1)
    chosen = jax.random.randint(jax.random.fold_in(key, 12), (), 0, DEVICES)
    counts = jnp.where(owners == chosen, SLOTS, counts)
    counts = jnp.where(device == owners, SLOTS, jnp.where(beside, counts, 0))
    order_keys = jax.random.split(jax.random.fold_in(key, 13), DEVICES * DEVICES)
    orders = jax.vmap(lambda one_key: jax.random.permutation(one_key, AB_DEV))(order_keys)
    orders = orders.reshape(DEVICES, DEVICES, AB_DEV)[:, :, :SLOTS]
    slot_index = jnp.arange(SLOTS)[None, None, :]
    return jnp.where(slot_index < counts[:, :, None], orders, -1).astype(jnp.int32)


def pattern_of(key):
    gx_count = NSX // SX
    gy_count = NSY // SY
    rows = jnp.arange(NBLK, dtype=jnp.int32)
    device = rows // AB_DEV
    within = rows % AB_DEV
    tile_x = device // gy_count
    tile_y = device % gy_count
    keys_x = jax.random.split(jax.random.fold_in(key, 31), DEVICES)
    keys_y = jax.random.split(jax.random.fold_in(key, 32), DEVICES)
    perm_x = jax.vmap(lambda one_key: jax.random.permutation(one_key, AB_DEV))(keys_x)
    perm_y = jax.vmap(lambda one_key: jax.random.permutation(one_key, AB_DEV))(keys_y)
    back_x = jnp.argsort(perm_x, axis=1)
    back_y = jnp.argsort(perm_y, axis=1)
    lower_x = jnp.maximum(device - gy_count, 0)
    lower_y = jnp.maximum(device - 1, 0)
    next_in = jnp.where(within + 1 < AB_DEV, rows + 1, -1)
    prev_in = jnp.where(within > 0, rows - 1, -1)
    up_x = jnp.where(tile_x + 1 < gx_count, (device + gy_count) * AB_DEV + perm_x[device, within], -1)
    down_x = jnp.where(tile_x > 0, lower_x * AB_DEV + back_x[lower_x, within], -1)
    up_y = jnp.where(tile_y + 1 < gy_count, (device + 1) * AB_DEV + perm_y[device, within], -1)
    down_y = jnp.where(tile_y > 0, lower_y * AB_DEV + back_y[lower_y, within], -1)
    return jnp.stack([rows, next_in, prev_in, up_x, down_x, up_y, down_y], axis=1).astype(jnp.int32)


def draw_send_blocks(key, part):
    return routing_of(key)


def draw_column_target(key, part):
    ids = routing_of(key)
    key = jax.random.fold_in(key, 21)
    counts = jnp.sum((ids >= 0).astype(jnp.int32), axis=2)
    gx_count = NSX // SX
    gy_count = NSY // SY
    across = jnp.arange(NSX, dtype=jnp.int32)[:, None]
    along = jnp.arange(NSY, dtype=jnp.int32)[None, :]
    tile_x = across // SX
    tile_y = along // SY
    local_x = across % SX
    local_y = along % SY
    device = tile_x * gy_count + tile_y
    band_x = max(1, SX // 8)
    band_y = max(1, SY // 8)
    owner = device + 0 * local_x
    owner = jnp.where((local_y < band_y) & (tile_y > 0), device - 1, owner)
    owner = jnp.where((local_y >= SY - band_y) & (tile_y + 1 < gy_count), device + 1, owner)
    owner = jnp.where((local_x < band_x) & (tile_x > 0), device - gy_count, owner)
    owner = jnp.where((local_x >= SX - band_x) & (tile_x + 1 < gx_count), device + gy_count, owner)
    owner = owner.astype(jnp.int32)
    reach = counts[device + 0 * local_x, owner]
    slot = jax.random.randint(jax.random.fold_in(key, 1), (NSX, NSY), 0, reach)
    cell = jax.random.randint(jax.random.fold_in(key, 2), (NSX, NSY), 0, BS)
    centre = (local_x == SX // 2) & (local_y == SY // 2)
    beside_centre = (local_x == SX // 2) & (local_y == SY // 2 - 1)
    slot = jnp.where(centre, SLOTS - 1, jnp.where(beside_centre, 0, slot))
    cell = jnp.where(centre, BS - 1, jnp.where(beside_centre, 0, cell))
    owner = jnp.where(centre | beside_centre, device + 0 * local_x, owner)
    return (owner * (SLOTS * BS) + slot * BS + cell).astype(jnp.int32)


def draw_block_pattern(key, part):
    return pattern_of(key)


def draw_aquifer_blocks(key, part):
    pattern = pattern_of(key)
    key = jax.random.fold_in(key, 41)
    diag_key = jax.random.fold_in(key, 7)
    eye = jnp.eye(BS, dtype=jnp.float32)
    spread = 0.2 / BS

    def noise(ident):
        return jax.random.uniform(jax.random.fold_in(key, ident), (BS, BS), jnp.float32, -spread, spread)

    def one_row(row):
        line = pattern[row]
        base = noise(row * 4 + 3)
        extra = jnp.exp(jax.random.uniform(jax.random.fold_in(diag_key, row), (BS,), jnp.float32, jnp.log(0.05), jnp.log(0.5)))
        centre = (base + base.T) * 0.5 * (1.0 - eye) + eye * (7.4 + extra)[:, None]
        blocks = [centre]
        for slot_index in range(1, 7):
            family = (slot_index - 1) // 2
            partner = jnp.maximum(line[slot_index], 0)
            if slot_index % 2 == 1:
                coupling = noise(row * 4 + family) - eye
            else:
                coupling = noise(partner * 4 + family).T - eye
            blocks.append(jnp.where(line[slot_index] >= 0, coupling, 0.0))
        return jnp.stack(blocks, axis=0)
    return lax.map(one_row, jnp.arange(NBLK, dtype=jnp.int32))


def block_scale(own_key, extent, cuts, smallest, largest):
    loudness, own = 1.0, jax.random.fold_in(own_key, 6)
    for position, parts in cuts:
        heights = jnp.exp(jax.random.uniform(jax.random.fold_in(own, position), (parts,), jnp.float32, smallest / len(cuts), largest / len(cuts)))
        loudness = loudness * jnp.repeat(heights, extent[position] // parts).reshape([-1 if axis == position else 1 for axis in range(len(extent))])
    return loudness


def scatter_about(stream_key, shape, width, most, cuts=(), kind=jnp.bfloat16):
    loudness = block_scale(stream_key, shape, cuts, -0.22, 0.18) if cuts else 1.0
    drawn = jax.random.normal(stream_key, shape, jnp.float32) * width * loudness
    return jnp.minimum(jnp.maximum(drawn, -most), most).astype(kind)


def setup_inputs(seed: int = 0) -> dict:
    arg_keys = jax.random.split(jax.random.key(seed), 11)
    water_content = jnp.clip(0.15 + 0.19999999 * jax.random.uniform(arg_keys[0], (NL, NSX, NSY), jnp.float32) ** block_scale(arg_keys[0], (NL, NSX, NSY), ((1, 8), (2, 4)), -0.2, 0.2), 0.15, 0.35)
    porosity = jnp.clip(0.4 + 0.099999994 * jax.random.uniform(arg_keys[1], (NSX, NSY), jnp.float32) ** block_scale(arg_keys[1], (NSX, NSY), ((0, 8), (1, 4)), -0.2, 0.2), 0.4, 0.5)
    conduct = jnp.clip(jnp.exp(math.log(0.5) - 2.3025851 * jax.random.uniform(arg_keys[2], (NSX, NSY), jnp.float32) ** block_scale(arg_keys[2], (NSX, NSY), ((0, 8), (1, 4)), -0.2, 0.2)), 0.05, 0.5)
    exponent = jnp.clip(3.0 + 3.0 * jax.random.uniform(arg_keys[3], (NSX, NSY), jnp.float32) ** block_scale(arg_keys[3], (NSX, NSY), ((0, 8), (1, 4)), -0.2, 0.2), 3.0, 6.0)
    infiltration = jnp.clip(jnp.exp(math.log(0.2) - 2.3025851 * jax.random.uniform(arg_keys[4], (NSX, NSY), jnp.float32) ** block_scale(arg_keys[4], (NSX, NSY), ((0, 8), (1, 4)), -0.2, 0.2)), 0.02, 0.2)
    column_target = draw_column_target(jax.random.fold_in(arg_keys[10], 71), 0)
    send_blocks = draw_send_blocks(jax.random.fold_in(arg_keys[10], 71), 0)
    prior_heads = scatter_about(arg_keys[7], (NBLK, BS), 1.0, 6.0, ((0, 32),), jnp.float32)
    block_pattern = draw_block_pattern(jax.random.fold_in(arg_keys[10], 71), 0)
    aquifer_blocks = draw_aquifer_blocks(jax.random.fold_in(arg_keys[10], 71), 0)
    return dict(water_content=water_content, porosity=porosity, conduct=conduct, exponent=exponent, infiltration=infiltration, column_target=column_target, send_blocks=send_blocks, prior_heads=prior_heads, block_pattern=block_pattern, aquifer_blocks=aquifer_blocks)


residual_content = 0.05


def soil_sweeps(water_content, porosity, conduct, exponent, infiltration):
    span = porosity - residual_content

    def layer(flux, content):
        saturation = (content - residual_content) / span
        conduct_now = conduct * jnp.exp(exponent * jnp.log(saturation))
        slope = exponent * conduct_now / (saturation * span)
        change = (flux - conduct_now) / (1.0 + slope)
        return conduct_now + slope * change, content + change

    recharge = jnp.zeros_like(infiltration)
    for sweep_index in range(SWEEPS):
        bottom, water_content = lax.scan(layer, infiltration, water_content)
        recharge = recharge + bottom
    return water_content, recharge


def apply_operator(field, block_pattern, aquifer_blocks):
    padded = jnp.concatenate([field, jnp.zeros((1, field.shape[1]), field.dtype)], axis=0)
    index = jnp.where(block_pattern < 0, field.shape[0], block_pattern).astype(jnp.int32)
    nearby = padded[index]
    return jnp.einsum("rkij,rkj->ri", aquifer_blocks, nearby, precision=lax.Precision.HIGHEST)


def reference(water_content, porosity, conduct, exponent, infiltration, column_target, send_blocks, prior_heads, block_pattern, aquifer_blocks):
    soil_water, recharge = soil_sweeps(water_content, porosity, conduct, exponent, infiltration)
    tile_x = jnp.arange(NSX, dtype=jnp.int32) // SX
    tile_y = jnp.arange(NSY, dtype=jnp.int32) // SY
    source = tile_x[:, None] * N_GY + tile_y[None, :]
    bins = source * (DEVICES * SLOTS * BS) + column_target
    partial_value = jax.ops.segment_sum(recharge.reshape(-1), bins.reshape(-1), num_segments=DEVICES * DEVICES * SLOTS * BS)
    owner = jnp.arange(DEVICES, dtype=jnp.int32)[None, :, None]
    rows = jnp.where(send_blocks >= 0, owner * AB_DEV + send_blocks, NBLK).astype(jnp.int32)
    cells = jax.ops.segment_sum(partial_value.reshape(-1, BS), rows.reshape(-1), num_segments=NBLK + 1)[:NBLK]
    rhs = prior_heads + (AB_DEV * BS / (SX * SY)) * cells
    heads = prior_heads
    residual = rhs - apply_operator(heads, block_pattern, aquifer_blocks)
    direction = residual
    norm_now = jnp.sum(residual * residual)
    for iteration in range(ITERS):
        image = apply_operator(direction, block_pattern, aquifer_blocks)
        step_size = norm_now / jnp.sum(direction * image)
        heads = heads + step_size * direction
        residual = residual - step_size * image
        norm_next = jnp.sum(residual * residual)
        direction = residual + (norm_next / norm_now) * direction
        norm_now = norm_next
    padded = jnp.concatenate([heads, jnp.zeros((1, BS), heads.dtype)], axis=0)
    slot_heads = padded[rows].reshape(DEVICES, DEVICES * SLOTS * BS)
    column_heads = slot_heads[source, column_target]
    return soil_water, heads, column_heads
```

```python
import functools

import jax
import jax.numpy as jnp
from jax import lax
from jax.experimental import pallas as pl
from jax.experimental.pallas import tpu as pltpu
from jax.sharding import PartitionSpec as P

SWEEPS = 8
RESIDUAL = 0.05
SIDES = 4
BOTH = ("gx", "gy")
F32 = jnp.float32


def partner_of(index, count, odd):
    other = ((index - odd) ^ 1) + odd
    return other, 0 <= index - odd and 0 <= other < count


def swaps(gx_count, gy_count):
    perms = []
    for axis, odd in ((1, 0), (1, 1), (0, 0), (0, 1)):
        perm = []
        for x in range(gx_count):
            for y in range(gy_count):
                if axis == 1:
                    other, fits = partner_of(y, gy_count, odd)
                    across = gy_count - 1 - y if gy_count % 2 == 0 else y
                    target = (x, other if fits else across)
                else:
                    other, fits = partner_of(x, gx_count, odd)
                    beside = y ^ 1 if gy_count % 2 == 0 and gx_count % 2 == 0 else y
                    target = (other, y) if fits else (x, beside)
                perm.append((x * gy_count + y, target[0] * gy_count + target[1]))
        perms.append(perm)
    return perms


def owners_here(gx_count, gy_count):
    x = lax.axis_index("gx")
    y = lax.axis_index("gy")

    def neighbour(index, count, odd, make):
        other = ((index - odd) ^ 1) + odd
        fits = (index >= odd) & (other < count)
        return jnp.where(fits, make(other), -1)

    along = lambda other: x * gy_count + other
    across = lambda other: other * gy_count + y
    return [
        x * gy_count + y,
        neighbour(y, gy_count, 0, along),
        neighbour(y, gy_count, 1, along),
        neighbour(x, gx_count, 0, across),
        neighbour(x, gx_count, 1, across),
    ]


def slot_keys(owner_ref, slots, rows):
    row = lax.broadcasted_iota(jnp.int32, (rows, 128), 0)
    keys = jnp.full((rows, 128), -1, jnp.int32)
    for k in range(SIDES + 1):
        owner = owner_ref[0, k]
        inside = (row >= k * slots) & (row < (k + 1) * slots) & (owner >= 0)
        keys = jnp.where(inside, owner * slots + row - k * slots, keys)
    return keys


def soil_kernel(
    own_blocks, slots, width,
    owner_ref, send_ref, pattern_ref,
    water_ref, porosity_ref, conduct_ref, exponent_ref, inflow_ref, target_ref, heads_ref,
    soil_ref, index_ref, own_ref, *rest,
):
    side_refs = rest[:SIDES]
    offset_ref, recharge_ref, totals_ref = rest[SIDES:]
    step = pl.program_id(0)
    steps = pl.num_programs(0)
    layers, rows, columns = water_ref.shape
    hi_rows = -(-(SIDES + 1) * slots // 8) * 8

    @pl.when(step == 0)
    def _():
        totals_ref[...] = jnp.zeros_like(totals_ref)

    exponent = exponent_ref[...]
    offset_ref[...] = jnp.log2(conduct_ref[...]) - exponent * jnp.log2(porosity_ref[...] - RESIDUAL)
    recharge_ref[...] = jnp.zeros_like(recharge_ref)
    soil_ref[...] = water_ref[...] - RESIDUAL

    def layer(flux, content):
        power = exponent_ref[...]
        conduct_now = jnp.exp2(power * jnp.log2(content) + offset_ref[...])
        steep = power * conduct_now
        share = (flux - conduct_now) * pl.reciprocal(content + steep)
        return conduct_now + steep * share, content + content * share

    pair = 2

    @pl.loop(0, SWEEPS // pair)
    def _(_):
        fluxes = [inflow_ref[...] for _ in range(pair)]
        for diagonal in range(layers + pair - 1):
            for sweep in range(pair):
                at = diagonal - sweep
                if 0 <= at < layers:
                    flux, content = layer(fluxes[sweep], soil_ref[at])
                    fluxes[sweep] = flux
                    soil_ref[at] = content
        recharge_ref[...] += fluxes[0] + fluxes[1]

    soil_ref[...] = soil_ref[...] + RESIDUAL

    keys = slot_keys(owner_ref, slots, hi_rows)
    keys = jnp.concatenate([keys] * (columns // 128), axis=1)
    cell = lax.broadcasted_iota(jnp.int32, (width, columns), 0)

    @pl.loop(0, rows)
    def _(row):
        target = target_ref[pl.ds(row, 1), :]
        value = recharge_ref[pl.ds(row, 1), :]
        cells = jnp.broadcast_to(target & (width - 1), (width, columns))
        one_hot = jnp.where(cells == cell, 1.0, 0.0).astype(jnp.bfloat16)
        high = value.astype(jnp.bfloat16).astype(F32)
        low = value - high
        hit = jnp.broadcast_to(target // width, (hi_rows, columns)) == keys
        spread = jnp.concatenate(
            [
                jnp.where(hit, jnp.broadcast_to(high, (hi_rows, columns)), 0.0),
                jnp.where(hit, jnp.broadcast_to(low, (hi_rows, columns)), 0.0),
            ],
            axis=0,
        ).astype(jnp.bfloat16)
        totals_ref[...] += lax.dot_general(
            one_hot, spread, (((1,), (1,)), ((), ())), preferred_element_type=F32
        )

    @pl.when(step == steps - 1)
    def _():
        totals = totals_ref[...]
        padded = jnp.concatenate([totals, jnp.zeros((width, 128 - totals.shape[1]), F32)], axis=1)
        turned = padded.T
        sums = turned[:hi_rows] + turned[hi_rows : 2 * hi_rows]
        block = lax.broadcasted_iota(jnp.int32, (own_blocks, width), 0)
        for k in range(SIDES + 1):
            owner = owner_ref[0, k]
            placed = jnp.zeros((own_blocks, width), F32)
            for slot in range(slots):
                ident = send_ref[0, jnp.maximum(owner, 0), slot]
                at = k * slots + slot
                placed = placed + jnp.where(block == ident, sums[at : at + 1], 0.0)
            if k == 0:
                own_ref[...] = placed
            else:
                side_refs[k - 1][0:own_blocks, :] = placed
                side_refs[k - 1][own_blocks : 2 * own_blocks, :] = heads_ref[...]
        for r in range(own_blocks):
            for k in range(pattern_ref.shape[1]):
                ident = pattern_ref[r, k]
                owner = ident // own_blocks
                place = (SIDES + 1) * own_blocks
                for side in range(SIDES + 1):
                    fits = (owner == owner_ref[0, side]) & (ident >= 0)
                    place = jnp.where(fits, side * own_blocks + ident % own_blocks, place)
                index_ref[r, k] = place


def operate(index_ref, blocks_ref, table_ref):
    own_blocks, most, width = blocks_ref.shape[:3]
    image = jnp.zeros((own_blocks, width), F32)
    row = lax.broadcasted_iota(jnp.int32, (own_blocks, 3 * width), 0)
    for r in range(own_blocks):
        total = jnp.zeros((width, width), F32)
        for k in range(most):
            total = total + blocks_ref[r, k] * table_ref[pl.ds(index_ref[r, k], 1), :]
        first = total.astype(jnp.bfloat16)
        rest = total - first.astype(F32)
        second = rest.astype(jnp.bfloat16)
        third = (rest - second.astype(F32)).astype(jnp.bfloat16)
        parts = jnp.concatenate([first, second, third], axis=1)
        ones = jnp.where(row == r, 1.0, 0.0).astype(jnp.bfloat16)
        image = image + lax.dot_general(
            ones, parts, (((1,), (1,)), ((), ())), preferred_element_type=F32
        )
    return image


def fill_table(table_ref, own, sides, own_blocks):
    table_ref[0:own_blocks, :] = own
    for k, side in enumerate(sides):
        table_ref[(k + 1) * own_blocks : (k + 2) * own_blocks, :] = side
    table_ref[(SIDES + 1) * own_blocks :, :] = jnp.zeros((own_blocks, own.shape[1]), F32)


def start_kernel(area, index_ref, blocks_ref, own_ref, heads_ref, *rest):
    side_refs, (residual_ref, table_ref) = rest[:SIDES], rest[SIDES:]
    own_blocks = heads_ref.shape[0]
    fill_table(table_ref, heads_ref[...], [s[own_blocks:, :] for s in side_refs], own_blocks)
    cells = own_ref[...]
    for side in side_refs:
        cells = cells + side[:own_blocks, :]
    residual_ref[...] = heads_ref[...] + area * cells - operate(index_ref, blocks_ref, table_ref)


def apply_kernel(index_ref, blocks_ref, field_ref, *rest):
    side_refs, (image_ref, table_ref) = rest[:SIDES], rest[SIDES:]
    fill_table(table_ref, field_ref[...], [s[...] for s in side_refs], field_ref.shape[0])
    image_ref[...] = operate(index_ref, blocks_ref, table_ref)


def whole_sum(values):
    return jnp.sum(jnp.sum(values, axis=0, keepdims=True), axis=1, keepdims=True)


def last_kernel(index_ref, blocks_ref, r_ref, w_ref, field_ref, *rest):
    side_refs, (sums_ref, table_ref) = rest[:SIDES], rest[SIDES:]
    fill_table(table_ref, field_ref[...], [s[...] for s in side_refs], field_ref.shape[0])
    z = operate(index_ref, blocks_ref, table_ref)
    r, w, v = r_ref[...], w_ref[...], field_ref[...]
    rr = whole_sum(r * r)
    ratio = whole_sum(w * w) / rr
    shift = jnp.where((ratio > 0.0) & (ratio < 1e30), jnp.sqrt(ratio), 1.0)
    inverse = 1.0 / shift
    w1 = w * inverse - r
    v1 = (v * inverse - w) * inverse
    z1 = ((z * inverse - v) * inverse) * inverse
    v2 = v1 - w1
    z2 = z1 - v1
    z3 = z2 - v2
    sums = [
        rr, shift,
        whole_sum(r * w1), whole_sum(w1 * w1), whole_sum(r * v2), whole_sum(w1 * v2), whole_sum(v2 * v2),
        whole_sum(r * z3), whole_sum(w1 * z3), whole_sum(v2 * z3),
    ]
    lane = lax.broadcasted_iota(jnp.int32, (1, 128), 1)
    packed = jnp.zeros((1, 128), F32)
    for position, value in enumerate(sums):
        packed = jnp.where(lane == position, value, packed)
    sums_ref[...] = jnp.broadcast_to(packed[None], sums_ref.shape)


def solve_step(all_sums):
    lane = lax.broadcasted_iota(jnp.int32, all_sums.shape, 1)

    def take(position):
        return jnp.sum(jnp.where(lane == position, all_sums, 0.0), axis=1, keepdims=True)

    rr, shift, rw, ww, rv, wv, vv, rz, wz, vz = [take(p) for p in range(10)]

    def over(values):
        return jnp.sum(values, axis=0, keepdims=True)

    m0 = over(rr)
    theta = over(shift * (rw + rr)) / m0
    ratio = shift / theta
    e = ratio - 1.0
    p2 = ratio * ratio
    p3 = p2 * ratio
    p4 = p2 * p2
    rw, ww, rv = rw * ratio, ww * p2, rv * p2
    wv, rz = wv * p3, rz * p3
    vv, wz = vv * p4, wz * p4
    vz = vz * (p4 * ratio)
    e2 = e * e
    twice = 2.0 * e
    new_w_r = rw + e * rr
    new_w_w = ww + e * rw
    new_v_r = rv + twice * rw + e2 * rr
    new_v_w = wv + twice * ww + e2 * rw
    new_v_v = vv + twice * wv + e2 * rv
    m1 = over(new_w_r)
    m2 = over(new_w_w + e * new_w_r)
    m3 = over(wv + e * rv + twice * new_w_w + e2 * new_w_r)
    m4 = over(new_v_v + twice * new_v_w + e2 * new_v_r)
    m5 = over(vz + twice * wz + e2 * rz + 3.0 * e * new_v_v + 3.0 * e2 * new_v_w + e * e2 * new_v_r)
    a00, a01, a02 = m0 + m1, m1 + m2, m2 + m3
    a11, a12, a22 = m2 + m3, m3 + m4, m4 + m5
    f1 = a01 / a00
    f2 = a02 / a00
    b11 = a11 - f1 * a01
    b12 = a12 - f1 * a02
    b22 = a22 - f2 * a02
    g1 = m1 - f1 * m0
    g2 = m2 - f2 * m0
    f3 = b12 / b11
    y2 = (g2 - f3 * g1) / (b22 - f3 * b12)
    y1 = (g1 - b12 * y2) / b11
    y0 = (m0 - a01 * y1 - a02 * y2) / a00
    inverse = 1.0 / theta
    y2 = y2 * inverse
    return (y0 - y1) * inverse + y2, (y1 * inverse - 2.0 * y2) * inverse, y2 * inverse * inverse


def heads_kernel(slots, owner_ref, send_ref, all_ref, target_ref, heads_ref, r_ref, w_ref, v_ref, *rest):
    sides = rest[: 4 * SIDES]
    heads_out, columns_out, table_ref, slot_ref, keys_ref = rest[4 * SIDES :]
    own_blocks, width = heads_ref.shape
    hi_rows = keys_ref.shape[0]
    weight_r, weight_w, weight_v = solve_step(all_ref[:, 0, :])

    def new_heads(heads, r, w, v):
        return heads + weight_r * r + weight_w * w + weight_v * v

    mine = new_heads(heads_ref[...], r_ref[...], w_ref[...], v_ref[...])
    heads_out[...] = mine
    table_ref[0:own_blocks, :] = mine
    for k in range(SIDES):
        old, r, w, v = sides[4 * k : 4 * k + 4]
        table_ref[(k + 1) * own_blocks : (k + 2) * own_blocks, :] = new_heads(
            old[own_blocks:, :], r[...], w[...], v[...]
        )
    for k in range(SIDES + 1):
        owner = jnp.maximum(owner_ref[0, k], 0)
        for slot in range(slots):
            ident = jnp.maximum(send_ref[0, owner, slot], 0)
            slot_ref[k * slots + slot : k * slots + slot + 1, :] = table_ref[
                pl.ds(k * own_blocks + ident, 1), :
            ]
    keys_ref[...] = slot_keys(owner_ref, slots, hi_rows)
    rows, columns = target_ref.shape
    entries = (SIDES + 1) * slots

    @pl.loop(0, rows // 8)
    def _(step):
        at = pl.multiple_of(step * 8, 8)
        for part in range(columns // 128):
            target = target_ref[pl.ds(at, 8), part * 128 : (part + 1) * 128]
            lanes = target & (width - 1)
            key = target // width
            found = jnp.zeros((8, 128), F32)
            for entry in range(entries):
                table = jnp.broadcast_to(slot_ref[entry : entry + 1, :], (8, 128))
                values = jnp.take_along_axis(table, lanes, axis=1, mode="promise_in_bounds")
                wanted = jnp.broadcast_to(keys_ref[entry : entry + 1, :], (8, 128))
                found = jnp.where(key == wanted, values, found)
            columns_out[pl.ds(at, 8), part * 128 : (part + 1) * 128] = found


VMEM = pl.BlockSpec(memory_space=pltpu.VMEM)
SMEM = pl.BlockSpec(memory_space=pltpu.SMEM)


def body(
    water_content,
    porosity,
    conduct,
    exponent,
    infiltration,
    column_target,
    send_blocks,
    prior_heads,
    block_pattern,
    aquifer_blocks,
    gx_count,
    gy_count,
):
    devices, slots = send_blocks.shape[1:]
    own_blocks, width = prior_heads.shape
    layers, rows, columns = water_content.shape
    most = block_pattern.shape[1]
    hi_rows = -(-(SIDES + 1) * slots // 8) * 8
    area = own_blocks * width / (rows * columns)
    perms = swaps(gx_count, gy_count)
    owners = jnp.stack(owners_here(gx_count, gy_count)).astype(jnp.int32).reshape(1, SIDES + 1)
    blocks = pltpu.with_memory_space_constraint(aquifer_blocks, pltpu.VMEM)
    in_hbm = lambda array: pltpu.with_memory_space_constraint(array, pltpu.HBM)
    field = jax.ShapeDtypeStruct((own_blocks, width), F32)
    two = jax.ShapeDtypeStruct((2 * own_blocks, width), F32)
    table = pltpu.VMEM(((SIDES + 2) * own_blocks, width), F32)

    def trade(array):
        return [lax.ppermute(array, BOTH, perm) for perm in perms]

    chunk = 16
    flat = pl.BlockSpec((chunk, columns), lambda i: (i, 0))
    deep = pl.BlockSpec((layers, chunk, columns), lambda i: (0, i, 0))
    whole = lambda shape: pl.BlockSpec(shape, lambda i: (0,) * len(shape))
    outs = pl.pallas_call(
        functools.partial(soil_kernel, own_blocks, slots, width),
        grid=(rows // chunk,),
        in_specs=[SMEM, SMEM, SMEM, deep, flat, flat, flat, flat, flat, whole((own_blocks, width))],
        out_specs=[deep, SMEM, whole((own_blocks, width))] + [whole((2 * own_blocks, width))] * SIDES,
        out_shape=[
            jax.ShapeDtypeStruct(water_content.shape, F32),
            jax.ShapeDtypeStruct((own_blocks, most), jnp.int32),
            field,
        ]
        + [two] * SIDES,
        scratch_shapes=[
            pltpu.VMEM((chunk, columns), F32),
            pltpu.VMEM((chunk, columns), F32),
            pltpu.VMEM((width, 2 * hi_rows), F32),
        ],
        compiler_params=pltpu.CompilerParams(vmem_limit_bytes=24 * 2**20),
        name="soil",
    )(
        owners, send_blocks, block_pattern,
        *map(in_hbm, (water_content, porosity, conduct, exponent, infiltration, column_target)),
        prior_heads,
    )
    soil_water, index, own = outs[:3]
    got = [lax.ppermute(out, BOTH, perm) for out, perm in zip(outs[3:], perms)]

    def small(kernel, args, shape, name):
        return pl.pallas_call(
            kernel,
            in_specs=[SMEM] + [VMEM] * (len(args) - 1),
            out_specs=VMEM,
            out_shape=shape,
            scratch_shapes=[table],
            compiler_params=pltpu.CompilerParams(vmem_limit_bytes=16 * 2**20),
            name=name,
        )(*args)

    r = small(functools.partial(start_kernel, area), (index, blocks, own, prior_heads, *got), field, "start")
    r_sides = trade(r)
    w = small(apply_kernel, (index, blocks, r, *r_sides), field, "once")
    w_sides = trade(w)
    v = small(apply_kernel, (index, blocks, w, *w_sides), field, "twice")
    v_sides = trade(v)
    sums = small(
        last_kernel, (index, blocks, r, w, v, *v_sides), jax.ShapeDtypeStruct((devices, 1, 128), F32), "sums"
    )
    all_sums = lax.all_to_all(sums, BOTH, 0, 0)
    sides = []
    for k in range(SIDES):
        sides += [got[k], r_sides[k], w_sides[k], v_sides[k]]
    heads, column_heads = pl.pallas_call(
        functools.partial(heads_kernel, slots),
        in_specs=[SMEM, SMEM] + [VMEM] * (6 + 4 * SIDES),
        out_specs=[VMEM, VMEM],
        out_shape=[field, jax.ShapeDtypeStruct((rows, columns), F32)],
        scratch_shapes=[
            pltpu.VMEM(((SIDES + 1) * own_blocks, width), F32),
            pltpu.VMEM((hi_rows, width), F32),
            pltpu.VMEM((hi_rows, width), jnp.int32),
        ],
        compiler_params=pltpu.CompilerParams(vmem_limit_bytes=16 * 2**20),
        name="heads",
    )(owners, send_blocks, all_sums, column_target, prior_heads, r, w, v, *sides)
    return soil_water, heads, column_heads


def solution(mesh):
    placed = (
        P(None, "gx", "gy"),
        P("gx", "gy"),
        P("gx", "gy"),
        P("gx", "gy"),
        P("gx", "gy"),
        P("gx", "gy"),
        P(("gx", "gy"), None, None),
        P(("gx", "gy"), None),
        P(("gx", "gy"), None),
        P(("gx", "gy"), None, None, None),
    )
    return jax.shard_map(
        functools.partial(body, gx_count=mesh.shape["gx"], gy_count=mesh.shape["gy"]),
        mesh=mesh,
        in_specs=placed,
        out_specs=(P(None, "gx", "gy"), P(("gx", "gy"), None), P("gx", "gy")),
        check_vma=False,
    )
```

```python
import functools
import math

import jax
import jax.numpy as jnp
from jax import lax
from jax.experimental import pallas as pl
from jax.experimental.pallas import tpu as pltpu
from jax.sharding import PartitionSpec as P

SWEEPS = 8
RESIDUAL = 0.05
SIDES = 4
BOTH = ("gx", "gy")
F32 = jnp.float32
BF16 = jnp.bfloat16


def partner_of(index, count, odd):
    other = ((index - odd) ^ 1) + odd
    return other, 0 <= index - odd and 0 <= other < count


def swaps(gx_count, gy_count):
    perms = []
    for axis, odd in ((1, 0), (1, 1), (0, 0), (0, 1)):
        perm = []
        for x in range(gx_count):
            for y in range(gy_count):
                if axis == 1:
                    other, fits = partner_of(y, gy_count, odd)
                    across = gy_count - 1 - y if gy_count % 2 == 0 else y
                    target = (x, other if fits else across)
                else:
                    other, fits = partner_of(x, gx_count, odd)
                    beside = y ^ 1 if gy_count % 2 == 0 and gx_count % 2 == 0 else y
                    target = (other, y) if fits else (x, beside)
                perm.append((x * gy_count + y, target[0] * gy_count + target[1]))
        perms.append(perm)
    return perms


def owners_here(gx_count, gy_count):
    x = lax.axis_index("gx")
    y = lax.axis_index("gy")

    def neighbour(index, count, odd, make):
        other = ((index - odd) ^ 1) + odd
        fits = (index >= odd) & (other < count)
        return jnp.where(fits, make(other), -1)

    along = lambda other: x * gy_count + other
    across = lambda other: other * gy_count + y
    return [
        x * gy_count + y,
        neighbour(y, gy_count, 0, along),
        neighbour(y, gy_count, 1, along),
        neighbour(x, gx_count, 0, across),
        neighbour(x, gx_count, 1, across),
    ]


def soil_tile(place, water_ref, porosity_ref, conduct_ref, exponent_ref, inflow_ref, soil_ref, recharge_ref):
    layers = water_ref.shape[0]
    power = exponent_ref[place]
    less = power - 1.0
    inverse = 1.0 / power
    kappa = jnp.exp2(
        (jnp.log2(power * conduct_ref[place]) - power * jnp.log2(porosity_ref[place] - RESIDUAL)) / less
    )
    back = 1.0 / kappa
    bend = less * (-0.5 * math.log(2.0))
    inflow = inflow_ref[place] * (kappa * power)

    def layer(flux, content):
        turn = jnp.tanh(bend * jnp.log2(content))
        whole = flux + content
        kept = whole * (0.5 + 0.5 * turn)
        return whole - kept, content + (kept - content) * inverse

    pair = 2
    total = None
    for first in range(0, SWEEPS, pair):
        fluxes = [inflow] * pair
        contents = [None] * layers
        for diagonal in range(layers + pair - 1):
            for sweep in reversed(range(pair)):
                at = diagonal - sweep
                if not 0 <= at < layers:
                    continue
                here = (at,) + place
                if sweep:
                    content = contents[at]
                elif first:
                    content = soil_ref[here]
                else:
                    content = (water_ref[here] - RESIDUAL) * kappa
                fluxes[sweep], content = layer(fluxes[sweep], content)
                contents[at] = content
                if sweep == pair - 1:
                    last = first + pair == SWEEPS
                    soil_ref[here] = content * back + RESIDUAL if last else content
        for flux in fluxes:
            total = flux if total is None else total + flux
    recharge_ref[place] = total * (back * inverse)


def bin_rows(target_ref, recharge_ref, keys, totals_ref, width):
    rows, columns = target_ref.shape
    slots_high = keys.shape[0]
    shift = width.bit_length() - 1
    keys = jnp.concatenate([keys] * (columns // 128), axis=1)
    cell = lax.broadcasted_iota(jnp.int32, (width, columns), 0).astype(F32).astype(BF16)
    target = target_ref[...]
    value = recharge_ref[...]
    cells = (target & (width - 1)).astype(F32)
    slot = lax.shift_right_logical(target, shift)
    high = value.astype(BF16).astype(F32)
    low = value - high
    one_hot = []
    spread = []
    for row in range(rows):
        line = slice(row, row + 1)
        wide = jnp.broadcast_to(cells[line], (16, columns)).astype(BF16)
        wide = jnp.concatenate([wide] * (width // 16), axis=0)
        one_hot.append(jnp.where(wide == cell, BF16(1), BF16(0)))
        hit = jnp.broadcast_to(slot[line], (slots_high, columns)) == keys
        parts = [
            jnp.where(hit, jnp.broadcast_to(part[line], (slots_high, columns)), 0.0) for part in (high, low)
        ]
        spread.append(jnp.concatenate(parts, axis=0).astype(BF16))
    totals_ref[...] += lax.dot_general(
        jnp.concatenate(spread, axis=1),
        jnp.concatenate(one_hot, axis=1),
        (((1,), (1,)), ((), ())),
        preferred_element_type=F32,
    )


def soil_kernel(
    gx_count, gy_count,
    water_ref, porosity_ref, conduct_ref, exponent_ref, inflow_ref, target_ref, heads_ref,
    send_hbm, pattern_hbm, blocks_hbm,
    soil_ref, index_ref, entry_ref, own_ref, *rest,
):
    side_refs = rest[:SIDES]
    blocks_out, recharge_ref, totals_ref, send_ref, pattern_ref, sems = rest[SIDES:]
    step = pl.program_id(0)
    steps = pl.num_programs(0)
    rows, columns = recharge_ref.shape
    own_blocks, width = heads_ref.shape
    slots = send_ref.shape[0]
    hi_rows = entry_ref.shape[1]
    owners = owners_here(gx_count, gy_count)
    copies = [
        pltpu.make_async_copy(send_hbm, send_ref, sems.at[0]),
        pltpu.make_async_copy(pattern_hbm, pattern_ref, sems.at[1]),
        pltpu.make_async_copy(blocks_hbm, blocks_out, sems.at[2]),
    ]

    @pl.when(step == 0)
    def _():
        for copy in copies:
            copy.start()
        totals_ref[...] = jnp.zeros_like(totals_ref)

    @pl.loop(0, rows // 8)
    def _(tile):
        place = (pl.ds(pl.multiple_of(tile * 8, 8), 8), slice(None))
        soil_tile(
            place, water_ref, porosity_ref, conduct_ref, exponent_ref, inflow_ref, soil_ref, recharge_ref
        )

    row = lax.broadcasted_iota(jnp.int32, (hi_rows, 128), 0)
    keys = jnp.full((hi_rows, 128), -1, jnp.int32)
    for k, owner in enumerate(owners):
        inside = (row >= k * slots) & (row < (k + 1) * slots) & (owner >= 0)
        keys = jnp.where(inside, owner * slots + row - k * slots, keys)
    bin_rows(target_ref, recharge_ref, keys, totals_ref, width)

    @pl.when(step == steps - 1)
    def _():
        for copy in copies:
            copy.wait()
        sums = totals_ref[0:hi_rows, :] + totals_ref[hi_rows : 2 * hi_rows, :]
        block = lax.broadcasted_iota(jnp.int32, (own_blocks, width), 0)
        for k, owner in enumerate(owners):
            out_ref = side_refs[k - 1] if k else own_ref
            placed = jnp.zeros((own_blocks, width), F32)
            for slot in range(slots):
                ident = send_ref[slot, jnp.maximum(owner, 0)]
                at = k * slots + slot
                placed = placed + jnp.where(block == ident, sums[at : at + 1], 0.0)
                entry_ref[0, at] = k * own_blocks + jnp.maximum(ident, 0)
                entry_ref[1, at] = jnp.where(owner >= 0, owner * slots + slot, -1)
            out_ref[0:own_blocks, :] = placed
            out_ref[own_blocks : 2 * own_blocks, :] = heads_ref[...]
        for r in range(own_blocks):
            for k in range(pattern_ref.shape[1]):
                ident = pattern_ref[r, k]
                owner = ident // own_blocks
                place = (SIDES + 1) * own_blocks
                for side in range(SIDES + 1):
                    fits = (owner == owners[side]) & (ident >= 0)
                    place = jnp.where(fits, side * own_blocks + ident % own_blocks, place)
                index_ref[r, k] = place


def operate(index_ref, blocks_ref, table_ref):
    own_blocks, most, width = blocks_ref.shape[:3]
    image = jnp.zeros((own_blocks, width), F32)
    row = lax.broadcasted_iota(jnp.int32, (own_blocks, 3 * width), 0)
    for r in range(own_blocks):
        total = jnp.zeros((width, width), F32)
        for k in range(most):
            total = total + blocks_ref[r, k] * table_ref[pl.ds(index_ref[r, k], 1), :]
        first = total.astype(jnp.bfloat16)
        rest = total - first.astype(F32)
        second = rest.astype(jnp.bfloat16)
        third = (rest - second.astype(F32)).astype(jnp.bfloat16)
        parts = jnp.concatenate([first, second, third], axis=1)
        ones = jnp.where(row == r, 1.0, 0.0).astype(jnp.bfloat16)
        image = image + lax.dot_general(
            ones, parts, (((1,), (1,)), ((), ())), preferred_element_type=F32
        )
    return image


def fill_table(table_ref, own, sides, own_blocks):
    table_ref[0:own_blocks, :] = own
    for k, side in enumerate(sides):
        table_ref[(k + 1) * own_blocks : (k + 2) * own_blocks, :] = side
    table_ref[(SIDES + 1) * own_blocks :, :] = jnp.zeros((own_blocks, own.shape[1]), F32)


def start_kernel(area, index_ref, blocks_ref, own_ref, *rest):
    side_refs, (residual_ref, table_ref) = rest[:SIDES], rest[SIDES:]
    own_blocks = residual_ref.shape[0]
    heads = own_ref[own_blocks:, :]
    fill_table(table_ref, heads, [s[own_blocks:, :] for s in side_refs], own_blocks)
    cells = own_ref[:own_blocks, :]
    for side in side_refs:
        cells = cells + side[:own_blocks, :]
    residual_ref[...] = heads + area * cells - operate(index_ref, blocks_ref, table_ref)


def apply_kernel(index_ref, blocks_ref, field_ref, *rest):
    side_refs, (image_ref, table_ref) = rest[:SIDES], rest[SIDES:]
    fill_table(table_ref, field_ref[...], [s[...] for s in side_refs], field_ref.shape[0])
    image_ref[...] = operate(index_ref, blocks_ref, table_ref)


def whole_sum(values):
    return jnp.sum(jnp.sum(values, axis=0, keepdims=True), axis=1, keepdims=True)


def last_kernel(index_ref, blocks_ref, r_ref, w_ref, field_ref, *rest):
    side_refs, (sums_ref, table_ref) = rest[:SIDES], rest[SIDES:]
    fill_table(table_ref, field_ref[...], [s[...] for s in side_refs], field_ref.shape[0])
    z = operate(index_ref, blocks_ref, table_ref)
    r, w, v = r_ref[...], w_ref[...], field_ref[...]
    rr = whole_sum(r * r)
    ratio = whole_sum(w * w) / rr
    shift = jnp.where((ratio > 0.0) & (ratio < 1e30), jnp.sqrt(ratio), 1.0)
    inverse = 1.0 / shift
    w1 = w * inverse - r
    v1 = (v * inverse - w) * inverse
    z1 = ((z * inverse - v) * inverse) * inverse
    v2 = v1 - w1
    z2 = z1 - v1
    z3 = z2 - v2
    sums = [
        rr, shift,
        whole_sum(r * w1), whole_sum(w1 * w1), whole_sum(r * v2), whole_sum(w1 * v2), whole_sum(v2 * v2),
        whole_sum(r * z3), whole_sum(w1 * z3), whole_sum(v2 * z3),
    ]
    lane = lax.broadcasted_iota(jnp.int32, (1, 128), 1)
    packed = jnp.zeros((1, 128), F32)
    for position, value in enumerate(sums):
        packed = jnp.where(lane == position, value, packed)
    sums_ref[...] = jnp.broadcast_to(packed[None], sums_ref.shape)


def solve_step(all_sums):
    lane = lax.broadcasted_iota(jnp.int32, all_sums.shape, 1)

    def take(position):
        return jnp.sum(jnp.where(lane == position, all_sums, 0.0), axis=1, keepdims=True)

    rr, shift, rw, ww, rv, wv, vv, rz, wz, vz = [take(p) for p in range(10)]

    def over(values):
        return jnp.sum(values, axis=0, keepdims=True)

    m0 = over(rr)
    theta = over(shift * (rw + rr)) / m0
    ratio = shift / theta
    e = ratio - 1.0
    p2 = ratio * ratio
    p3 = p2 * ratio
    p4 = p2 * p2
    rw, ww, rv = rw * ratio, ww * p2, rv * p2
    wv, rz = wv * p3, rz * p3
    vv, wz = vv * p4, wz * p4
    vz = vz * (p4 * ratio)
    e2 = e * e
    twice = 2.0 * e
    new_w_r = rw + e * rr
    new_w_w = ww + e * rw
    new_v_r = rv + twice * rw + e2 * rr
    new_v_w = wv + twice * ww + e2 * rw
    new_v_v = vv + twice * wv + e2 * rv
    m1 = over(new_w_r)
    m2 = over(new_w_w + e * new_w_r)
    m3 = over(wv + e * rv + twice * new_w_w + e2 * new_w_r)
    m4 = over(new_v_v + twice * new_v_w + e2 * new_v_r)
    m5 = over(vz + twice * wz + e2 * rz + 3.0 * e * new_v_v + 3.0 * e2 * new_v_w + e * e2 * new_v_r)
    a00, a01, a02 = m0 + m1, m1 + m2, m2 + m3
    a11, a12, a22 = m2 + m3, m3 + m4, m4 + m5
    f1 = a01 / a00
    f2 = a02 / a00
    b11 = a11 - f1 * a01
    b12 = a12 - f1 * a02
    b22 = a22 - f2 * a02
    g1 = m1 - f1 * m0
    g2 = m2 - f2 * m0
    f3 = b12 / b11
    y2 = (g2 - f3 * g1) / (b22 - f3 * b12)
    y1 = (g1 - b12 * y2) / b11
    y0 = (m0 - a01 * y1 - a02 * y2) / a00
    inverse = 1.0 / theta
    y2 = y2 * inverse
    return (y0 - y1) * inverse + y2, (y1 * inverse - 2.0 * y2) * inverse, y2 * inverse * inverse


def heads_kernel(slots, entry_ref, all_ref, target_ref, own_ref, r_ref, w_ref, v_ref, *rest):
    sides = rest[: 4 * SIDES]
    heads_out, columns_out, table_ref, slot_ref = rest[4 * SIDES :]
    own_blocks, width = r_ref.shape
    shift = width.bit_length() - 1
    weight_r, weight_w, weight_v = solve_step(all_ref[:, 0, :])

    def new_heads(old, r, w, v):
        return old[own_blocks:, :] + weight_r * r[...] + weight_w * w[...] + weight_v * v[...]

    mine = new_heads(own_ref, r_ref, w_ref, v_ref)
    heads_out[...] = mine
    table_ref[0:own_blocks, :] = mine
    for k in range(SIDES):
        table_ref[(k + 1) * own_blocks : (k + 2) * own_blocks, :] = new_heads(*sides[4 * k : 4 * k + 4])
    entries = (SIDES + 1) * slots
    for entry in range(entries):
        slot_ref[entry] = jnp.broadcast_to(table_ref[pl.ds(entry_ref[0, entry], 1), :], (8, width))
    rows, columns = target_ref.shape

    @pl.loop(0, rows // 8)
    def _(step):
        at = pl.multiple_of(step * 8, 8)
        for part in range(columns // 128):
            here = (pl.ds(at, 8), slice(part * 128, (part + 1) * 128))
            target = target_ref[here]
            lanes = target & (width - 1)
            key = lax.shift_right_logical(target, shift)
            found = jnp.zeros((8, 128), F32)
            for entry in range(entries):
                values = jnp.take_along_axis(slot_ref[entry], lanes, axis=1, mode="promise_in_bounds")
                found = jnp.where(key == entry_ref[1, entry], values, found)
            columns_out[here] = found


VMEM = pl.BlockSpec(memory_space=pltpu.VMEM)
SMEM = pl.BlockSpec(memory_space=pltpu.SMEM)
ANY = pl.BlockSpec(memory_space=pl.ANY)


def body(
    water_content,
    porosity,
    conduct,
    exponent,
    infiltration,
    column_target,
    send_blocks,
    prior_heads,
    block_pattern,
    aquifer_blocks,
    gx_count,
    gy_count,
):
    devices, slots = send_blocks.shape[1:]
    own_blocks, width = prior_heads.shape
    layers, rows, columns = water_content.shape
    most = block_pattern.shape[1]
    hi_rows = -(-(SIDES + 1) * slots // 8) * 8
    area = own_blocks * width / (rows * columns)
    perms = swaps(gx_count, gy_count)
    in_hbm = lambda array: pltpu.with_memory_space_constraint(array, pltpu.HBM)
    field = jax.ShapeDtypeStruct((own_blocks, width), F32)
    two = jax.ShapeDtypeStruct((2 * own_blocks, width), F32)
    table = pltpu.VMEM(((SIDES + 2) * own_blocks, width), F32)

    def trade(array):
        return [lax.ppermute(array, BOTH, perm) for perm in perms]

    chunk = 16
    flat = pl.BlockSpec((chunk, columns), lambda i: (i, 0))
    deep = pl.BlockSpec((layers, chunk, columns), lambda i: (0, i, 0))
    whole = lambda shape: pl.BlockSpec(shape, lambda i: (0,) * len(shape))
    outs = pl.pallas_call(
        functools.partial(soil_kernel, gx_count, gy_count),
        grid=(rows // chunk,),
        in_specs=[deep, flat, flat, flat, flat, flat, whole((own_blocks, width)), ANY, ANY, ANY],
        out_specs=[deep, SMEM, SMEM] + [whole((2 * own_blocks, width))] * (SIDES + 1) + [ANY],
        out_shape=[
            jax.ShapeDtypeStruct(water_content.shape, F32),
            jax.ShapeDtypeStruct((own_blocks, most), jnp.int32),
            jax.ShapeDtypeStruct((2, hi_rows), jnp.int32),
        ]
        + [two] * (SIDES + 1)
        + [pltpu.VMEM(aquifer_blocks.shape, F32)],
        scratch_shapes=[
            pltpu.VMEM((chunk, columns), F32),
            pltpu.VMEM((2 * hi_rows, width), F32),
            pltpu.SMEM((slots, devices), jnp.int32),
            pltpu.SMEM(block_pattern.shape, jnp.int32),
            pltpu.SemaphoreType.DMA((3,)),
        ],
        compiler_params=pltpu.CompilerParams(vmem_limit_bytes=24 * 2**20),
        name="soil",
    )(
        *map(
            in_hbm,
            (
                water_content, porosity, conduct, exponent, infiltration, column_target, prior_heads,
                send_blocks[0].T, block_pattern, aquifer_blocks,
            ),
        )
    )
    soil_water, index, entries, own = outs[:4]
    blocks = pltpu.with_memory_space_constraint(outs[-1], pltpu.VMEM)
    got = [lax.ppermute(out, BOTH, perm) for out, perm in zip(outs[4:], perms)]

    def small(kernel, args, shape, name):
        return pl.pallas_call(
            kernel,
            in_specs=[SMEM] + [VMEM] * (len(args) - 1),
            out_specs=VMEM,
            out_shape=shape,
            scratch_shapes=[table],
            compiler_params=pltpu.CompilerParams(vmem_limit_bytes=16 * 2**20),
            name=name,
        )(*args)

    r = small(functools.partial(start_kernel, area), (index, blocks, own, *got), field, "start")
    r_sides = trade(r)
    w = small(apply_kernel, (index, blocks, r, *r_sides), field, "once")
    w_sides = trade(w)
    v = small(apply_kernel, (index, blocks, w, *w_sides), field, "twice")
    v_sides = trade(v)
    sums = small(
        last_kernel, (index, blocks, r, w, v, *v_sides), jax.ShapeDtypeStruct((devices, 1, 128), F32), "sums"
    )
    all_sums = lax.all_to_all(sums, BOTH, 0, 0)
    sides = []
    for k in range(SIDES):
        sides += [got[k], r_sides[k], w_sides[k], v_sides[k]]
    heads, column_heads = pl.pallas_call(
        functools.partial(heads_kernel, slots),
        in_specs=[SMEM] + [VMEM] * (6 + 4 * SIDES),
        out_specs=[VMEM, VMEM],
        out_shape=[field, jax.ShapeDtypeStruct((rows, columns), F32)],
        scratch_shapes=[
            pltpu.VMEM(((SIDES + 1) * own_blocks, width), F32),
            pltpu.VMEM((hi_rows, 8, width), F32),
        ],
        compiler_params=pltpu.CompilerParams(vmem_limit_bytes=16 * 2**20),
        name="heads",
    )(entries, all_sums, column_target, own, r, w, v, *sides)
    return soil_water, heads, column_heads


def solution(mesh):
    placed = (
        P(None, "gx", "gy"),
        P("gx", "gy"),
        P("gx", "gy"),
        P("gx", "gy"),
        P("gx", "gy"),
        P("gx", "gy"),
        P(("gx", "gy"), None, None),
        P(("gx", "gy"), None),
        P(("gx", "gy"), None),
        P(("gx", "gy"), None, None, None),
    )
    return jax.shard_map(
        functools.partial(body, gx_count=mesh.shape["gx"], gy_count=mesh.shape["gy"]),
        mesh=mesh,
        in_specs=placed,
        out_specs=(P(None, "gx", "gy"), P(("gx", "gy"), None), P("gx", "gy")),
        check_vma=False,
    )
```

```python
import functools
import math

import jax
import jax.numpy as jnp
from jax import lax
from jax.experimental import pallas as pl
from jax.experimental.pallas import tpu as pltpu
from jax.sharding import PartitionSpec as P

SWEEPS = 8
RESIDUAL = 0.05
SIDES = 4
BOTH = ("gx", "gy")
ORDER = ((0, 1), (1, 1), (0, 0), (1, 0))
F32 = jnp.float32
BF16 = jnp.bfloat16


def partner_of(index, count, odd):
    other = ((index - odd) ^ 1) + odd
    return other, 0 <= index - odd and 0 <= other < count


def swaps(gx_count, gy_count):
    perms = []
    for axis, odd in ORDER:
        perm = []
        for x in range(gx_count):
            for y in range(gy_count):
                if axis == 1:
                    other, fits = partner_of(y, gy_count, odd)
                    across = gy_count - 1 - y if gy_count % 2 == 0 else y
                    target = (x, other if fits else across)
                else:
                    other, fits = partner_of(x, gx_count, odd)
                    beside = y ^ 1 if gy_count % 2 == 0 and gx_count % 2 == 0 else y
                    target = (other, y) if fits else (x, beside)
                perm.append((x * gy_count + y, target[0] * gy_count + target[1]))
        perms.append(perm)
    return perms


def owners_here(gx_count, gy_count):
    x = lax.axis_index("gx")
    y = lax.axis_index("gy")

    def neighbour(index, count, odd, make):
        other = ((index - odd) ^ 1) + odd
        fits = (index >= odd) & (other < count)
        return jnp.where(fits, make(other), -1)

    along = lambda other: x * gy_count + other
    across = lambda other: other * gy_count + y
    found = [x * gy_count + y]
    for axis, odd in ORDER:
        found.append(neighbour(y, gy_count, odd, along) if axis else neighbour(x, gx_count, odd, across))
    return found


def soil_tile(place, water_ref, porosity_ref, conduct_ref, exponent_ref, inflow_ref, recharge_ref):
    layers = water_ref.shape[0]
    power = exponent_ref[place]
    less = power - 1.0
    inverse = 1.0 / power
    kappa = jnp.exp2(
        (jnp.log2(power * conduct_ref[place]) - power * jnp.log2(porosity_ref[place] - RESIDUAL)) / less
    )
    back = 1.0 / kappa
    bend = less * (0.5 * math.log(2.0))
    inflow = inflow_ref[place] * (kappa * power)

    def layer(flux, content):
        turn = jnp.tanh(bend * jnp.log2(content))
        below = (flux + content) * (0.5 + 0.5 * turn)
        return below, content + (flux - below) * inverse

    pair = 2
    total = None
    for first in range(0, SWEEPS, pair):
        fluxes = [inflow] * pair
        contents = [None] * layers
        for diagonal in range(layers + pair - 1):
            for sweep in reversed(range(pair)):
                at = diagonal - sweep
                if not 0 <= at < layers:
                    continue
                here = (at,) + place
                if sweep:
                    content = contents[at]
                elif first:
                    content = water_ref[here]
                else:
                    content = (water_ref[here] - RESIDUAL) * kappa
                fluxes[sweep], content = layer(fluxes[sweep], content)
                contents[at] = content
                if sweep == pair - 1:
                    last = first + pair == SWEEPS
                    water_ref[here] = content * back + RESIDUAL if last else content
        for flux in fluxes:
            total = flux if total is None else total + flux
    recharge_ref[place] = total * (back * inverse)


def bin_rows(target, value, keys, totals_ref, width):
    rows, columns = target.shape
    slots_high = keys.shape[0]
    shift = width.bit_length() - 1
    keys = jnp.concatenate([keys] * (columns // 128), axis=1)
    cell = lax.broadcasted_iota(jnp.int32, (width, columns), 0).astype(F32).astype(BF16)
    cells = (target & (width - 1)).astype(F32)
    slot = lax.shift_right_logical(target, shift)
    high = value.astype(BF16).astype(F32)
    low = value - high
    one_hot = []
    spread = []
    for row in range(rows):
        line = slice(row, row + 1)
        wide = jnp.broadcast_to(cells[line], (16, columns)).astype(BF16)
        wide = jnp.concatenate([wide] * (width // 16), axis=0)
        one_hot.append(jnp.where(wide == cell, BF16(1), BF16(0)))
        hit = jnp.broadcast_to(slot[line], (slots_high, columns)) == keys
        parts = [
            jnp.where(hit, jnp.broadcast_to(part[line], (slots_high, columns)), 0.0) for part in (high, low)
        ]
        spread.append(jnp.concatenate(parts, axis=0).astype(BF16))
    totals_ref[...] += lax.dot_general(
        jnp.concatenate(spread, axis=1),
        jnp.concatenate(one_hot, axis=1),
        (((1,), (1,)), ((), ())),
        preferred_element_type=F32,
    )


def prepare(gx_count, gy_count, send, pattern, own_blocks, source_ref, block_ref, key_ref):
    hi_rows, width = key_ref.shape
    slots, devices = send.shape
    owners = owners_here(gx_count, gy_count)
    row = lax.broadcasted_iota(jnp.int32, (hi_rows, width), 0)
    keys = jnp.full((hi_rows, width), -1, jnp.int32)
    for k, owner in enumerate(owners):
        inside = (row >= k * slots) & (row < (k + 1) * slots) & (owner >= 0)
        keys = jnp.where(inside, owner * slots + row - k * slots, keys)
    key_ref[...] = keys
    lane = lax.broadcasted_iota(jnp.int32, (slots, devices), 1)
    block_ref[...] = jnp.full(block_ref.shape, -1, jnp.int32)
    for k, owner in enumerate(owners):
        idents = jnp.sum(jnp.where(lane == owner, send, 0), axis=1, keepdims=True)
        block_ref[k, 0:slots, :] = jnp.broadcast_to(idents, (slots, width))
    shift = own_blocks.bit_length() - 1
    most = pattern.shape[1]
    for k in range(most):
        ident = jnp.broadcast_to(pattern[:, k : k + 1], (own_blocks, width))
        side = jnp.full((own_blocks, width), -1, jnp.int32)
        for at, owner in enumerate(owners):
            side = jnp.where((lax.shift_right_arithmetic(ident, shift) == owner) & (ident >= 0), at, side)
        source_ref[k] = side
        source_ref[most + k] = ident & (own_blocks - 1)


def soil_kernel(
    gx_count, gy_count,
    water_hbm, porosity_hbm, conduct_hbm, exponent_hbm, inflow_hbm, target_hbm, heads_hbm,
    send_hbm, pattern_hbm, blocks_hbm,
    soil_hbm, source_ref, block_ref, key_ref, own_ref, *rest,
):
    side_refs = rest[:SIDES]
    (
        blocks_out, water_ref, porosity_ref, conduct_ref, exponent_ref, inflow_ref, target_ref,
        heads_ref, send_ref, pattern_ref, recharge_ref, totals_ref, small_sems, in_sems, out_sems, blocks_sem,
    ) = rest[SIDES:]
    rows, columns = recharge_ref.shape
    own_blocks, width = heads_ref.shape
    slots = send_ref.shape[0]
    hi_rows = key_ref.shape[0]
    chunks = in_sems.shape[0]
    chunk = rows // chunks
    flats = (
        (porosity_hbm, porosity_ref), (conduct_hbm, conduct_ref), (exponent_hbm, exponent_ref),
        (inflow_hbm, inflow_ref), (target_hbm, target_ref),
    )

    def small_copies():
        pairs = ((send_hbm, send_ref), (pattern_hbm, pattern_ref), (heads_hbm, heads_ref))
        return [pltpu.make_async_copy(a, b, small_sems.at[at]) for at, (a, b) in enumerate(pairs)]

    def incoming(at):
        here = (pl.ds(pl.multiple_of(at * chunk, 8), chunk), slice(None))
        deep = (slice(None),) + here
        copies = [pltpu.make_async_copy(a.at[here], b.at[here], in_sems.at[at, f]) for f, (a, b) in enumerate(flats)]
        return copies + [pltpu.make_async_copy(water_hbm.at[deep], water_ref.at[deep], in_sems.at[at, len(flats)])]

    def outgoing(at):
        deep = (slice(None), pl.ds(pl.multiple_of(at * chunk, 8), chunk), slice(None))
        return pltpu.make_async_copy(water_ref.at[deep], soil_hbm.at[deep], out_sems.at[at])

    blocks_copy = pltpu.make_async_copy(blocks_hbm, blocks_out, blocks_sem)
    for copy in small_copies() + incoming(0) + incoming(1):
        copy.start()
    totals_ref[...] = jnp.zeros_like(totals_ref)
    for copy in small_copies():
        copy.wait()
    prepare(
        gx_count, gy_count, send_ref[...], pattern_ref[...], own_blocks, source_ref, block_ref, key_ref
    )

    @pl.loop(0, chunks)
    def _(at):
        for copy in incoming(at):
            copy.wait()

        @pl.when(at + 2 < chunks)
        def _():
            for copy in incoming(at + 2):
                copy.start()

        @pl.when(at == chunks - 2)
        def _():
            blocks_copy.start()

        @pl.loop(0, chunk // 8)
        def _(tile):
            place = (pl.ds(pl.multiple_of(at * chunk + tile * 8, 8), 8), slice(None))
            soil_tile(place, water_ref, porosity_ref, conduct_ref, exponent_ref, inflow_ref, recharge_ref)

        outgoing(at).start()
        here = (pl.ds(pl.multiple_of(at * chunk, 8), chunk), slice(None))
        bin_rows(target_ref[here], recharge_ref[here], key_ref[...], totals_ref, width)

    sums = totals_ref[0:hi_rows, :] + totals_ref[hi_rows : 2 * hi_rows, :]
    block = lax.broadcasted_iota(jnp.int32, (own_blocks, width), 0)
    for k in range(SIDES + 1):
        out_ref = side_refs[k - 1] if k else own_ref
        idents = block_ref[k]
        placed = jnp.zeros((own_blocks, width), F32)
        for slot in range(slots):
            at = k * slots + slot
            placed = placed + jnp.where(block == idents[slot : slot + 1], sums[at : at + 1], 0.0)
        out_ref[0:own_blocks, :] = placed
        out_ref[own_blocks : 2 * own_blocks, :] = heads_ref[...]
    blocks_copy.wait()

    @pl.loop(0, chunks)
    def _(at):
        outgoing(at).wait()


def operate(source_ref, blocks_ref, fields):
    own_blocks, most, width = blocks_ref.shape[:3]
    nearby = []
    for k in range(most):
        side, line = source_ref[k], source_ref[most + k]
        rows = jnp.zeros((own_blocks, width), F32)
        for at, field in enumerate(fields):
            picked = jnp.take_along_axis(field, line, axis=0, mode="promise_in_bounds")
            rows = jnp.where(side == at, picked, rows)
        nearby.append(rows)
    image = jnp.zeros((own_blocks, width), F32)
    row = lax.broadcasted_iota(jnp.int32, (own_blocks, 3 * width), 0)
    for r in range(own_blocks):
        total = blocks_ref[r, 0] * nearby[0][r : r + 1]
        for k in range(1, most):
            total = total + blocks_ref[r, k] * nearby[k][r : r + 1]
        first = total.astype(BF16)
        rest = total - first.astype(F32)
        second = rest.astype(BF16)
        third = (rest - second.astype(F32)).astype(BF16)
        parts = jnp.concatenate([first, second, third], axis=1)
        ones = jnp.where(row == r, 1.0, 0.0).astype(BF16)
        image = image + lax.dot_general(
            ones, parts, (((1,), (1,)), ((), ())), preferred_element_type=F32
        )
    return image


def start_kernel(area, source_ref, blocks_ref, own_ref, *rest):
    side_refs, residual_ref = rest[:SIDES][::-1], rest[SIDES]
    own_blocks = residual_ref.shape[0]
    heads = own_ref[own_blocks:, :]
    cells = own_ref[:own_blocks, :]
    for side in side_refs:
        cells = cells + side[:own_blocks, :]
    fields = [heads] + [s[own_blocks:, :] for s in side_refs]
    residual_ref[...] = heads + area * cells - operate(source_ref, blocks_ref, fields)


def apply_kernel(source_ref, blocks_ref, *rest):
    image_ref = rest[-1]
    fields = [f[...] for f in (rest[0],) + rest[-2:0:-1]]
    image_ref[...] = operate(source_ref, blocks_ref, fields)


def whole_sum(values):
    return jnp.sum(jnp.sum(values, axis=0, keepdims=True), axis=1, keepdims=True)


def last_kernel(source_ref, blocks_ref, r_ref, w_ref, *rest):
    fields, sums_ref = [f[...] for f in (rest[0],) + rest[-2:0:-1]], rest[-1]
    z = operate(source_ref, blocks_ref, fields)
    r, w, v = r_ref[...], w_ref[...], fields[0]
    rr = whole_sum(r * r)
    ratio = whole_sum(w * w) / rr
    shift = jnp.where((ratio > 0.0) & (ratio < 1e30), jnp.sqrt(ratio), 1.0)
    inverse = 1.0 / shift
    w1 = w * inverse - r
    v1 = (v * inverse - w) * inverse
    z1 = ((z * inverse - v) * inverse) * inverse
    v2 = v1 - w1
    z2 = z1 - v1
    z3 = z2 - v2
    sums = [
        rr, shift,
        whole_sum(r * w1), whole_sum(w1 * w1), whole_sum(r * v2), whole_sum(w1 * v2), whole_sum(v2 * v2),
        whole_sum(r * z3), whole_sum(w1 * z3), whole_sum(v2 * z3),
    ]
    lane = lax.broadcasted_iota(jnp.int32, (1, 128), 1)
    packed = jnp.zeros((1, 128), F32)
    for position, value in enumerate(sums):
        packed = jnp.where(lane == position, value, packed)
    sums_ref[...] = jnp.broadcast_to(packed[None], sums_ref.shape)


def solve_step(all_sums):
    lane = lax.broadcasted_iota(jnp.int32, all_sums.shape, 1)

    def take(position):
        return jnp.sum(jnp.where(lane == position, all_sums, 0.0), axis=1, keepdims=True)

    rr, shift, rw, ww, rv, wv, vv, rz, wz, vz = [take(p) for p in range(10)]

    def over(values):
        return jnp.sum(values, axis=0, keepdims=True)

    m0 = over(rr)
    theta = over(shift * (rw + rr)) / m0
    ratio = shift / theta
    e = ratio - 1.0
    p2 = ratio * ratio
    p3 = p2 * ratio
    p4 = p2 * p2
    rw, ww, rv = rw * ratio, ww * p2, rv * p2
    wv, rz = wv * p3, rz * p3
    vv, wz = vv * p4, wz * p4
    vz = vz * (p4 * ratio)
    e2 = e * e
    twice = 2.0 * e
    new_w_r = rw + e * rr
    new_w_w = ww + e * rw
    new_v_r = rv + twice * rw + e2 * rr
    new_v_w = wv + twice * ww + e2 * rw
    new_v_v = vv + twice * wv + e2 * rv
    m1 = over(new_w_r)
    m2 = over(new_w_w + e * new_w_r)
    m3 = over(wv + e * rv + twice * new_w_w + e2 * new_w_r)
    m4 = over(new_v_v + twice * new_v_w + e2 * new_v_r)
    m5 = over(vz + twice * wz + e2 * rz + 3.0 * e * new_v_v + 3.0 * e2 * new_v_w + e * e2 * new_v_r)
    a00, a01, a02 = m0 + m1, m1 + m2, m2 + m3
    a11, a12, a22 = m2 + m3, m3 + m4, m4 + m5
    f1 = a01 / a00
    f2 = a02 / a00
    b11 = a11 - f1 * a01
    b12 = a12 - f1 * a02
    b22 = a22 - f2 * a02
    g1 = m1 - f1 * m0
    g2 = m2 - f2 * m0
    f3 = b12 / b11
    y2 = (g2 - f3 * g1) / (b22 - f3 * b12)
    y1 = (g1 - b12 * y2) / b11
    y0 = (m0 - a01 * y1 - a02 * y2) / a00
    inverse = 1.0 / theta
    y2 = y2 * inverse
    return (y0 - y1) * inverse + y2, (y1 * inverse - 2.0 * y2) * inverse, y2 * inverse * inverse


def heads_kernel(slots, block_ref, key_ref, all_ref, target_ref, own_ref, r_ref, w_ref, v_ref, *rest):
    sides = rest[: 4 * SIDES]
    heads_hbm, columns_hbm, slot_ref, heads_ref, columns_ref, sems = rest[4 * SIDES :]
    own_blocks, width = r_ref.shape
    shift = width.bit_length() - 1
    weight_r, weight_w, weight_v = solve_step(all_ref[:, 0, :])

    def new_heads(old, r, w, v):
        return old[own_blocks:, :] + weight_r * r[...] + weight_w * w[...] + weight_v * v[...]

    heads_copy = pltpu.make_async_copy(heads_ref, heads_hbm, sems.at[0])
    for k in range(SIDES + 1):
        four = sides[4 * k - 4 : 4 * k] if k else (own_ref, r_ref, w_ref, v_ref)
        heads = new_heads(*four)
        if k == 0:
            heads_ref[...] = heads
            heads_copy.start()
        lines = jnp.maximum(block_ref[k], 0)
        picked = jnp.take_along_axis(heads, lines, axis=0, mode="promise_in_bounds")
        for slot in range(slots):
            slot_ref[k * slots + slot] = jnp.broadcast_to(picked[slot : slot + 1], (8, width))
    entries = (SIDES + 1) * slots
    rows, columns = target_ref.shape
    copies = []
    for at in range(0, rows, 8):
        for part in range(0, columns, 128):
            here = (slice(at, at + 8), slice(part, part + 128))
            target = target_ref[here]
            lanes = target & (width - 1)
            key = lax.shift_right_logical(target, shift)
            found = jnp.zeros((8, 128), F32)
            for entry in range(entries):
                values = jnp.take_along_axis(slot_ref[entry], lanes, axis=1, mode="promise_in_bounds")
                wanted = jnp.broadcast_to(key_ref[entry : entry + 1, :], (8, 128))
                found = jnp.where(key == wanted, values, found)
            columns_ref[here] = found
        if (at + 8) % 16 == 0:
            here = (slice(at - 8, at + 8), slice(None))
            copies.append(
                pltpu.make_async_copy(columns_ref.at[here], columns_hbm.at[here], sems.at[1 + len(copies)])
            )
            copies[-1].start()
    heads_copy.wait()
    for copy in copies:
        copy.wait()


VMEM = pl.BlockSpec(memory_space=pltpu.VMEM)
ANY = pl.BlockSpec(memory_space=pl.ANY)


def body(
    water_content,
    porosity,
    conduct,
    exponent,
    infiltration,
    column_target,
    send_blocks,
    prior_heads,
    block_pattern,
    aquifer_blocks,
    gx_count,
    gy_count,
):
    devices, slots = send_blocks.shape[1:]
    own_blocks, width = prior_heads.shape
    layers, rows, columns = water_content.shape
    most = block_pattern.shape[1]
    hi_rows = -(-(SIDES + 1) * slots // 8) * 8
    area = own_blocks * width / (rows * columns)
    perms = swaps(gx_count, gy_count)
    in_hbm = lambda array: pltpu.with_memory_space_constraint(array, pltpu.HBM)
    field = jax.ShapeDtypeStruct((own_blocks, width), F32)
    two = jax.ShapeDtypeStruct((2 * own_blocks, width), F32)

    def trade(array):
        return [lax.ppermute(array, BOTH, perm) for perm in perms]

    chunks = rows // 16
    outs = pl.pallas_call(
        functools.partial(soil_kernel, gx_count, gy_count),
        in_specs=[ANY] * 10,
        out_specs=[ANY] + [VMEM] * (SIDES + 4) + [ANY],
        out_shape=[
            jax.ShapeDtypeStruct(water_content.shape, F32),
            jax.ShapeDtypeStruct((2 * most, own_blocks, width), jnp.int32),
            jax.ShapeDtypeStruct((SIDES + 1, own_blocks, width), jnp.int32),
            jax.ShapeDtypeStruct((hi_rows, width), jnp.int32),
        ]
        + [two] * (SIDES + 1)
        + [pltpu.VMEM(aquifer_blocks.shape, F32)],
        scratch_shapes=[
            pltpu.VMEM(water_content.shape, F32),
            *[pltpu.VMEM((rows, columns), F32)] * 4,
            pltpu.VMEM((rows, columns), jnp.int32),
            pltpu.VMEM((own_blocks, width), F32),
            pltpu.VMEM((slots, devices), jnp.int32),
            pltpu.VMEM((own_blocks, most), jnp.int32),
            pltpu.VMEM((rows, columns), F32),
            pltpu.VMEM((2 * hi_rows, width), F32),
            pltpu.SemaphoreType.DMA((3,)),
            pltpu.SemaphoreType.DMA((chunks, 6)),
            pltpu.SemaphoreType.DMA((chunks,)),
            pltpu.SemaphoreType.DMA,
        ],
        compiler_params=pltpu.CompilerParams(vmem_limit_bytes=24 * 2**20),
        name="soil",
    )(
        *map(
            in_hbm,
            (
                water_content, porosity, conduct, exponent, infiltration, column_target, prior_heads,
                send_blocks[0].T, block_pattern, aquifer_blocks,
            ),
        )
    )
    soil_water, source, block, key, own = outs[:5]
    blocks = pltpu.with_memory_space_constraint(outs[-1], pltpu.VMEM)
    got = [lax.ppermute(out, BOTH, perm) for out, perm in zip(outs[5:], perms)]

    def small(kernel, args, shape, name):
        return pl.pallas_call(
            kernel,
            in_specs=[VMEM] * (2 + len(args)),
            out_specs=VMEM,
            out_shape=shape,
            compiler_params=pltpu.CompilerParams(vmem_limit_bytes=16 * 2**20),
            name=name,
        )(source, blocks, *args)

    r = small(functools.partial(start_kernel, area), (own, *got[::-1]), field, "start")
    r_sides = trade(r)
    w = small(apply_kernel, (r, *r_sides[::-1]), field, "once")
    w_sides = trade(w)
    v = small(apply_kernel, (w, *w_sides[::-1]), field, "twice")
    v_sides = trade(v)
    sums = small(last_kernel, (r, w, v, *v_sides[::-1]), jax.ShapeDtypeStruct((devices, 1, width), F32), "sums")
    all_sums = lax.all_to_all(sums, BOTH, 0, 0)
    sides = []
    for k in range(SIDES):
        sides += [got[k], r_sides[k], w_sides[k], v_sides[k]]
    heads, column_heads = pl.pallas_call(
        functools.partial(heads_kernel, slots),
        in_specs=[VMEM] * (8 + 4 * SIDES),
        out_specs=[ANY, ANY],
        out_shape=[field, jax.ShapeDtypeStruct((rows, columns), F32)],
        scratch_shapes=[
            pltpu.VMEM((hi_rows, 8, width), F32),
            pltpu.VMEM((own_blocks, width), F32),
            pltpu.VMEM((rows, columns), F32),
            pltpu.SemaphoreType.DMA((1 + rows // 16,)),
        ],
        compiler_params=pltpu.CompilerParams(vmem_limit_bytes=16 * 2**20),
        name="heads",
    )(block, key, all_sums, column_target, own, r, w, v, *sides)
    return soil_water, heads, column_heads


def solution(mesh):
    placed = (
        P(None, "gx", "gy"),
        P("gx", "gy"),
        P("gx", "gy"),
        P("gx", "gy"),
        P("gx", "gy"),
        P("gx", "gy"),
        P(("gx", "gy"), None, None),
        P(("gx", "gy"), None),
        P(("gx", "gy"), None),
        P(("gx", "gy"), None, None, None),
    )
    return jax.shard_map(
        functools.partial(body, gx_count=mesh.shape["gx"], gy_count=mesh.shape["gy"]),
        mesh=mesh,
        in_specs=placed,
        out_specs=(P(None, "gx", "gy"), P(("gx", "gy"), None), P("gx", "gy")),
        check_vma=False,
    )
```

```python
import functools
import math

import jax
import jax.numpy as jnp
from jax import lax
from jax.experimental import pallas as pl
from jax.experimental.pallas import tpu as pltpu
from jax.sharding import PartitionSpec as P

SWEEPS = 8
RESIDUAL = 0.05
SIDES = 4
BOTH = ("gx", "gy")
ORDER = ((0, 1), (1, 1), (0, 0), (1, 0))
F32 = jnp.float32
BF16 = jnp.bfloat16


def partner_of(index, count, odd):
    other = ((index - odd) ^ 1) + odd
    return other, 0 <= index - odd and 0 <= other < count


def swaps(gx_count, gy_count):
    perms = []
    for axis, odd in ORDER:
        perm = []
        for x in range(gx_count):
            for y in range(gy_count):
                if axis == 1:
                    other, fits = partner_of(y, gy_count, odd)
                    across = gy_count - 1 - y if gy_count % 2 == 0 else y
                    target = (x, other if fits else across)
                else:
                    other, fits = partner_of(x, gx_count, odd)
                    beside = y ^ 1 if gy_count % 2 == 0 and gx_count % 2 == 0 else y
                    target = (other, y) if fits else (x, beside)
                perm.append((x * gy_count + y, target[0] * gy_count + target[1]))
        perms.append(perm)
    return perms


def owners_here(gx_count, gy_count):
    x = lax.axis_index("gx")
    y = lax.axis_index("gy")

    def neighbour(index, count, odd, make):
        other = ((index - odd) ^ 1) + odd
        fits = (index >= odd) & (other < count)
        return jnp.where(fits, make(other), -1)

    along = lambda other: x * gy_count + other
    across = lambda other: other * gy_count + y
    found = [x * gy_count + y]
    for axis, odd in ORDER:
        found.append(neighbour(y, gy_count, odd, along) if axis else neighbour(x, gx_count, odd, across))
    return found


def soil_tile(place, water_ref, porosity_ref, conduct_ref, exponent_ref, inflow_ref):
    layers = water_ref.shape[0]
    power = exponent_ref[place]
    less = power - 1.0
    inverse = 1.0 / power
    kappa = jnp.exp2(
        (jnp.log2(power * conduct_ref[place]) - power * jnp.log2(porosity_ref[place] - RESIDUAL)) / less
    )
    back = 1.0 / kappa
    bend = less * (0.5 * math.log(2.0))
    inflow = inflow_ref[place] * (kappa * power)

    def layer(flux, content):
        turn = jnp.tanh(bend * jnp.log2(content))
        below = (flux + content) * (0.5 + 0.5 * turn)
        return below, content + (flux - below) * inverse

    pair = 2
    total = None
    for first in range(0, SWEEPS, pair):
        fluxes = [inflow] * pair
        contents = [None] * layers
        for diagonal in range(layers + pair - 1):
            for sweep in reversed(range(pair)):
                at = diagonal - sweep
                if not 0 <= at < layers:
                    continue
                here = (at,) + place
                if sweep:
                    content = contents[at]
                elif first:
                    content = water_ref[here]
                else:
                    content = (water_ref[here] - RESIDUAL) * kappa
                fluxes[sweep], content = layer(fluxes[sweep], content)
                contents[at] = content
                if sweep == pair - 1:
                    last = first + pair == SWEEPS
                    water_ref[here] = content * back + RESIDUAL if last else content
        for flux in fluxes:
            total = flux if total is None else total + flux
    return total * (back * inverse)


def bin_rows(target, value, keys, totals_ref, width):
    rows, columns = target.shape
    slots_high = keys.shape[0]
    shift = width.bit_length() - 1
    keys = jnp.concatenate([keys] * (columns // 128), axis=1)
    cell = lax.broadcasted_iota(jnp.int32, (width, columns), 0).astype(F32).astype(BF16)
    cells = (target & (width - 1)).astype(F32)
    slot = lax.shift_right_logical(target, shift)
    high = value.astype(BF16).astype(F32)
    low = value - high
    one_hot = []
    spread = []
    for row in range(rows):
        line = slice(row, row + 1)
        wide = jnp.broadcast_to(cells[line], (16, columns)).astype(BF16)
        wide = jnp.concatenate([wide] * (width // 16), axis=0)
        one_hot.append(jnp.where(wide == cell, BF16(1), BF16(0)))
        hit = jnp.broadcast_to(slot[line], (slots_high, columns)) == keys
        parts = [
            jnp.where(hit, jnp.broadcast_to(part[line], (slots_high, columns)), 0.0) for part in (high, low)
        ]
        spread.append(jnp.concatenate(parts, axis=0).astype(BF16))
    totals_ref[...] += lax.dot_general(
        jnp.concatenate(spread, axis=1),
        jnp.concatenate(one_hot, axis=1),
        (((1,), (1,)), ((), ())),
        preferred_element_type=F32,
    )


def prepare(gx_count, gy_count, send, pattern, own_blocks, source_ref, block_ref, key_ref):
    hi_rows, width = key_ref.shape
    slots, devices = send.shape
    owners = owners_here(gx_count, gy_count)
    row = lax.broadcasted_iota(jnp.int32, (hi_rows, width), 0)
    keys = jnp.full((hi_rows, width), -1, jnp.int32)
    for k, owner in enumerate(owners):
        inside = (row >= k * slots) & (row < (k + 1) * slots) & (owner >= 0)
        keys = jnp.where(inside, owner * slots + row - k * slots, keys)
    key_ref[...] = keys
    lane = lax.broadcasted_iota(jnp.int32, (slots, devices), 1)
    block_ref[...] = jnp.full(block_ref.shape, -1, jnp.int32)
    for k, owner in enumerate(owners):
        idents = jnp.sum(jnp.where(lane == owner, send, 0), axis=1, keepdims=True)
        block_ref[k, 0:slots, :] = jnp.broadcast_to(idents, (slots, width))
    shift = own_blocks.bit_length() - 1
    most = pattern.shape[1]
    for k in range(most):
        ident = jnp.broadcast_to(pattern[:, k : k + 1], (own_blocks, width))
        side = jnp.full((own_blocks, width), -1, jnp.int32)
        for at, owner in enumerate(owners):
            side = jnp.where((lax.shift_right_arithmetic(ident, shift) == owner) & (ident >= 0), at, side)
        source_ref[k] = side
        source_ref[most + k] = ident & (own_blocks - 1)


def soil_kernel(
    gx_count, gy_count,
    water_hbm, porosity_hbm, conduct_hbm, exponent_hbm, inflow_hbm, target_hbm, heads_hbm,
    send_hbm, pattern_hbm, blocks_hbm,
    soil_hbm, source_ref, block_ref, key_ref, own_ref, *rest,
):
    side_refs = rest[:SIDES]
    (
        blocks_out, water_ref, porosity_ref, conduct_ref, exponent_ref, inflow_ref, target_ref,
        heads_ref, send_ref, pattern_ref, recharge_ref, totals_ref, small_sems, in_sems, out_sems, blocks_sem,
    ) = rest[SIDES:]
    rows, columns = target_ref.shape
    own_blocks, width = heads_ref.shape
    slots = send_ref.shape[0]
    hi_rows = key_ref.shape[0]
    chunks = in_sems.shape[0]
    chunk = rows // chunks
    flats = (
        (porosity_hbm, porosity_ref), (conduct_hbm, conduct_ref), (exponent_hbm, exponent_ref),
        (inflow_hbm, inflow_ref), (target_hbm, target_ref),
    )

    def small_copies():
        pairs = ((send_hbm, send_ref), (pattern_hbm, pattern_ref), (heads_hbm, heads_ref))
        return [pltpu.make_async_copy(a, b, small_sems.at[at]) for at, (a, b) in enumerate(pairs)]

    def incoming(at):
        here = (pl.ds(pl.multiple_of(at * chunk, 8), chunk), slice(None))
        deep = (slice(None),) + here
        copies = [pltpu.make_async_copy(a.at[here], b.at[here], in_sems.at[at, f]) for f, (a, b) in enumerate(flats)]
        return copies + [pltpu.make_async_copy(water_hbm.at[deep], water_ref.at[deep], in_sems.at[at, len(flats)])]

    def outgoing(at):
        deep = (slice(None), pl.ds(pl.multiple_of(at * chunk, 8), chunk), slice(None))
        return pltpu.make_async_copy(water_ref.at[deep], soil_hbm.at[deep], out_sems.at[at])

    blocks_copy = pltpu.make_async_copy(blocks_hbm, blocks_out, blocks_sem)
    for copy in small_copies() + incoming(0) + incoming(1):
        copy.start()
    totals_ref[...] = jnp.zeros_like(totals_ref)
    recharge_ref[0:8, :] = jnp.zeros((8, columns), F32)
    for copy in small_copies():
        copy.wait()
    prepare(
        gx_count, gy_count, send_ref[...], pattern_ref[...], own_blocks, source_ref, block_ref, key_ref
    )

    def bin_tile(tile):
        target = target_ref[pl.ds(pl.multiple_of(jnp.maximum(tile, 0) * 8, 8), 8), :]
        value = recharge_ref[pl.ds(pl.multiple_of(tile * 8 + 8, 8), 8), :]
        bin_rows(target, value, key_ref[...], totals_ref, width)

    @pl.loop(0, chunks)
    def _(at):
        for copy in incoming(at):
            copy.wait()

        @pl.when(at + 2 < chunks)
        def _():
            for copy in incoming(at + 2):
                copy.start()

        @pl.when(at == chunks - 2)
        def _():
            blocks_copy.start()

        @pl.loop(0, chunk // 8)
        def _(tile):
            tile = at * (chunk // 8) + tile
            bin_tile(tile - 1)
            place = (pl.ds(pl.multiple_of(tile * 8, 8), 8), slice(None))
            recharge_ref[pl.ds(pl.multiple_of(tile * 8 + 8, 8), 8), :] = soil_tile(
                place, water_ref, porosity_ref, conduct_ref, exponent_ref, inflow_ref
            )

        outgoing(at).start()

    bin_tile(rows // 8 - 1)
    sums = totals_ref[0:hi_rows, :] + totals_ref[hi_rows : 2 * hi_rows, :]
    block = lax.broadcasted_iota(jnp.int32, (own_blocks, width), 0)
    for k in range(SIDES + 1):
        out_ref = side_refs[k - 1] if k else own_ref
        idents = block_ref[k]
        placed = jnp.zeros((own_blocks, width), F32)
        for slot in range(slots):
            at = k * slots + slot
            placed = placed + jnp.where(block == idents[slot : slot + 1], sums[at : at + 1], 0.0)
        out_ref[0:own_blocks, :] = placed
        out_ref[own_blocks : 2 * own_blocks, :] = heads_ref[...]
    blocks_copy.wait()

    @pl.loop(0, chunks)
    def _(at):
        outgoing(at).wait()


def operate(source_ref, blocks_ref, fields):
    own_blocks, most, width = blocks_ref.shape[:3]
    nearby = []
    for k in range(most):
        side, line = source_ref[k], source_ref[most + k]
        rows = jnp.zeros((own_blocks, width), F32)
        for at, field in enumerate(fields):
            picked = jnp.take_along_axis(field, line, axis=0, mode="promise_in_bounds")
            rows = jnp.where(side == at, picked, rows)
        nearby.append(rows)
    image = jnp.zeros((own_blocks, width), F32)
    row = lax.broadcasted_iota(jnp.int32, (own_blocks, 3 * width), 0)
    for r in range(own_blocks):
        total = blocks_ref[r, 0] * nearby[0][r : r + 1]
        for k in range(1, most):
            total = total + blocks_ref[r, k] * nearby[k][r : r + 1]
        first = total.astype(BF16)
        rest = total - first.astype(F32)
        second = rest.astype(BF16)
        third = (rest - second.astype(F32)).astype(BF16)
        parts = jnp.concatenate([first, second, third], axis=1)
        ones = jnp.where(row == r, 1.0, 0.0).astype(BF16)
        image = image + lax.dot_general(
            ones, parts, (((1,), (1,)), ((), ())), preferred_element_type=F32
        )
    return image


def start_kernel(area, source_ref, blocks_ref, own_ref, *rest):
    side_refs, residual_ref = rest[:SIDES], rest[SIDES]
    own_blocks = residual_ref.shape[0]
    heads = own_ref[own_blocks:, :]
    cells = own_ref[:own_blocks, :]
    for side in side_refs:
        cells = cells + side[:own_blocks, :]
    fields = [heads] + [s[own_blocks:, :] for s in side_refs]
    residual_ref[...] = heads + area * cells - operate(source_ref, blocks_ref, fields)


def apply_kernel(source_ref, blocks_ref, *rest):
    image_ref = rest[-1]
    fields = [f[...] for f in (rest[0],) + rest[-2:0:-1]]
    image_ref[...] = operate(source_ref, blocks_ref, fields)


def whole_sum(values):
    return jnp.sum(jnp.sum(values, axis=0, keepdims=True), axis=1, keepdims=True)


def last_kernel(source_ref, blocks_ref, r_ref, w_ref, *rest):
    fields, sums_ref = [f[...] for f in (rest[0],) + rest[-2:0:-1]], rest[-1]
    z = operate(source_ref, blocks_ref, fields)
    r, w, v = r_ref[...], w_ref[...], fields[0]
    rr = whole_sum(r * r)
    ratio = whole_sum(w * w) / rr
    shift = jnp.where((ratio > 0.0) & (ratio < 1e30), jnp.sqrt(ratio), 1.0)
    inverse = 1.0 / shift
    w1 = w * inverse - r
    v1 = (v * inverse - w) * inverse
    z1 = ((z * inverse - v) * inverse) * inverse
    v2 = v1 - w1
    z2 = z1 - v1
    z3 = z2 - v2
    sums = [
        rr, shift,
        whole_sum(r * w1), whole_sum(w1 * w1), whole_sum(r * v2), whole_sum(w1 * v2), whole_sum(v2 * v2),
        whole_sum(r * z3), whole_sum(w1 * z3), whole_sum(v2 * z3),
    ]
    lane = lax.broadcasted_iota(jnp.int32, (1, 128), 1)
    packed = jnp.zeros((1, 128), F32)
    for position, value in enumerate(sums):
        packed = jnp.where(lane == position, value, packed)
    sums_ref[...] = jnp.broadcast_to(packed[None], sums_ref.shape)


def solve_step(all_sums):
    lane = lax.broadcasted_iota(jnp.int32, all_sums.shape, 1)

    def take(position):
        return jnp.sum(jnp.where(lane == position, all_sums, 0.0), axis=1, keepdims=True)

    rr, shift, rw, ww, rv, wv, vv, rz, wz, vz = [take(p) for p in range(10)]

    def over(values):
        return jnp.sum(values, axis=0, keepdims=True)

    m0 = over(rr)
    theta = over(shift * (rw + rr)) / m0
    ratio = shift / theta
    e = ratio - 1.0
    p2 = ratio * ratio
    p3 = p2 * ratio
    p4 = p2 * p2
    rw, ww, rv = rw * ratio, ww * p2, rv * p2
    wv, rz = wv * p3, rz * p3
    vv, wz = vv * p4, wz * p4
    vz = vz * (p4 * ratio)
    e2 = e * e
    twice = 2.0 * e
    new_w_r = rw + e * rr
    new_w_w = ww + e * rw
    new_v_r = rv + twice * rw + e2 * rr
    new_v_w = wv + twice * ww + e2 * rw
    new_v_v = vv + twice * wv + e2 * rv
    m1 = over(new_w_r)
    m2 = over(new_w_w + e * new_w_r)
    m3 = over(wv + e * rv + twice * new_w_w + e2 * new_w_r)
    m4 = over(new_v_v + twice * new_v_w + e2 * new_v_r)
    m5 = over(vz + twice * wz + e2 * rz + 3.0 * e * new_v_v + 3.0 * e2 * new_v_w + e * e2 * new_v_r)
    a00, a01, a02 = m0 + m1, m1 + m2, m2 + m3
    a11, a12, a22 = m2 + m3, m3 + m4, m4 + m5
    f1 = a01 / a00
    f2 = a02 / a00
    b11 = a11 - f1 * a01
    b12 = a12 - f1 * a02
    b22 = a22 - f2 * a02
    g1 = m1 - f1 * m0
    g2 = m2 - f2 * m0
    f3 = b12 / b11
    y2 = (g2 - f3 * g1) / (b22 - f3 * b12)
    y1 = (g1 - b12 * y2) / b11
    y0 = (m0 - a01 * y1 - a02 * y2) / a00
    inverse = 1.0 / theta
    y2 = y2 * inverse
    return (y0 - y1) * inverse + y2, (y1 * inverse - 2.0 * y2) * inverse, y2 * inverse * inverse


def heads_kernel(slots, block_ref, key_ref, all_ref, target_ref, own_ref, r_ref, w_ref, v_ref, *rest):
    sides = rest[: 4 * SIDES]
    heads_hbm, columns_hbm, slot_ref, heads_ref, columns_ref, sems = rest[4 * SIDES :]
    own_blocks, width = r_ref.shape
    shift = width.bit_length() - 1
    weight_r, weight_w, weight_v = solve_step(all_ref[:, 0, :])

    def new_heads(old, r, w, v):
        return old[own_blocks:, :] + weight_r * r[...] + weight_w * w[...] + weight_v * v[...]

    heads_copy = pltpu.make_async_copy(heads_ref, heads_hbm, sems.at[0])
    for k in range(SIDES + 1):
        four = sides[4 * k - 4 : 4 * k] if k else (own_ref, r_ref, w_ref, v_ref)
        heads = new_heads(*four)
        if k == 0:
            heads_ref[...] = heads
            heads_copy.start()
        lines = jnp.maximum(block_ref[k], 0)
        picked = jnp.take_along_axis(heads, lines, axis=0, mode="promise_in_bounds")
        for slot in range(slots):
            slot_ref[k * slots + slot] = jnp.broadcast_to(picked[slot : slot + 1], (8, width))
    entries = (SIDES + 1) * slots
    rows, columns = target_ref.shape
    copies = []
    for at in range(0, rows, 8):
        for part in range(0, columns, 128):
            here = (slice(at, at + 8), slice(part, part + 128))
            target = target_ref[here]
            lanes = target & (width - 1)
            key = lax.shift_right_logical(target, shift)
            found = jnp.zeros((8, 128), F32)
            for entry in range(entries):
                values = jnp.take_along_axis(slot_ref[entry], lanes, axis=1, mode="promise_in_bounds")
                wanted = jnp.broadcast_to(key_ref[entry : entry + 1, :], (8, 128))
                found = jnp.where(key == wanted, values, found)
            columns_ref[here] = found
        if (at + 8) % 16 == 0:
            here = (slice(at - 8, at + 8), slice(None))
            copies.append(
                pltpu.make_async_copy(columns_ref.at[here], columns_hbm.at[here], sems.at[1 + len(copies)])
            )
            copies[-1].start()
    heads_copy.wait()
    for copy in copies:
        copy.wait()


VMEM = pl.BlockSpec(memory_space=pltpu.VMEM)
ANY = pl.BlockSpec(memory_space=pl.ANY)


def body(
    water_content,
    porosity,
    conduct,
    exponent,
    infiltration,
    column_target,
    send_blocks,
    prior_heads,
    block_pattern,
    aquifer_blocks,
    gx_count,
    gy_count,
):
    devices, slots = send_blocks.shape[1:]
    own_blocks, width = prior_heads.shape
    layers, rows, columns = water_content.shape
    most = block_pattern.shape[1]
    hi_rows = -(-(SIDES + 1) * slots // 8) * 8
    area = own_blocks * width / (rows * columns)
    perms = swaps(gx_count, gy_count)
    in_hbm = lambda array: pltpu.with_memory_space_constraint(array, pltpu.HBM)
    field = jax.ShapeDtypeStruct((own_blocks, width), F32)
    two = jax.ShapeDtypeStruct((2 * own_blocks, width), F32)

    def trade(array):
        return [lax.ppermute(array, BOTH, perm) for perm in perms]

    chunks = rows // 16
    outs = pl.pallas_call(
        functools.partial(soil_kernel, gx_count, gy_count),
        in_specs=[ANY] * 10,
        out_specs=[ANY] + [VMEM] * (SIDES + 4) + [ANY],
        out_shape=[
            jax.ShapeDtypeStruct(water_content.shape, F32),
            jax.ShapeDtypeStruct((2 * most, own_blocks, width), jnp.int32),
            jax.ShapeDtypeStruct((SIDES + 1, own_blocks, width), jnp.int32),
            jax.ShapeDtypeStruct((hi_rows, width), jnp.int32),
        ]
        + [two] * (SIDES + 1)
        + [pltpu.VMEM(aquifer_blocks.shape, F32)],
        scratch_shapes=[
            pltpu.VMEM(water_content.shape, F32),
            *[pltpu.VMEM((rows, columns), F32)] * 4,
            pltpu.VMEM((rows, columns), jnp.int32),
            pltpu.VMEM((own_blocks, width), F32),
            pltpu.VMEM((slots, devices), jnp.int32),
            pltpu.VMEM((own_blocks, most), jnp.int32),
            pltpu.VMEM((rows + 8, columns), F32),
            pltpu.VMEM((2 * hi_rows, width), F32),
            pltpu.SemaphoreType.DMA((3,)),
            pltpu.SemaphoreType.DMA((chunks, 6)),
            pltpu.SemaphoreType.DMA((chunks,)),
            pltpu.SemaphoreType.DMA,
        ],
        compiler_params=pltpu.CompilerParams(vmem_limit_bytes=24 * 2**20),
        name="soil",
    )(
        *map(
            in_hbm,
            (
                water_content, porosity, conduct, exponent, infiltration, column_target, prior_heads,
                send_blocks[0].T, block_pattern, aquifer_blocks,
            ),
        )
    )
    soil_water, source, block, key, own = outs[:5]
    blocks = pltpu.with_memory_space_constraint(outs[-1], pltpu.VMEM)
    got = [lax.ppermute(out, BOTH, perm) for out, perm in zip(outs[5:], perms)]

    def small(kernel, args, shape, name):
        return pl.pallas_call(
            kernel,
            in_specs=[VMEM] * (2 + len(args)),
            out_specs=VMEM,
            out_shape=shape,
            compiler_params=pltpu.CompilerParams(vmem_limit_bytes=16 * 2**20),
            name=name,
        )(source, blocks, *args)

    r = small(functools.partial(start_kernel, area), (own, *got), field, "start")
    r_sides = trade(r)
    w = small(apply_kernel, (r, *r_sides[::-1]), field, "once")
    w_sides = trade(w)
    v = small(apply_kernel, (w, *w_sides[::-1]), field, "twice")
    v_sides = trade(v)
    sums = small(last_kernel, (r, w, v, *v_sides[::-1]), jax.ShapeDtypeStruct((devices, 1, width), F32), "sums")
    all_sums = lax.all_to_all(sums, BOTH, 0, 0)
    sides = []
    for k in range(SIDES):
        sides += [got[k], r_sides[k], w_sides[k], v_sides[k]]
    heads, column_heads = pl.pallas_call(
        functools.partial(heads_kernel, slots),
        in_specs=[VMEM] * (8 + 4 * SIDES),
        out_specs=[ANY, ANY],
        out_shape=[field, jax.ShapeDtypeStruct((rows, columns), F32)],
        scratch_shapes=[
            pltpu.VMEM((hi_rows, 8, width), F32),
            pltpu.VMEM((own_blocks, width), F32),
            pltpu.VMEM((rows, columns), F32),
            pltpu.SemaphoreType.DMA((1 + rows // 16,)),
        ],
        compiler_params=pltpu.CompilerParams(vmem_limit_bytes=16 * 2**20),
        name="heads",
    )(block, key, all_sums, column_target, own, r, w, v, *sides)
    return soil_water, heads, column_heads


def solution(mesh):
    placed = (
        P(None, "gx", "gy"),
        P("gx", "gy"),
        P("gx", "gy"),
        P("gx", "gy"),
        P("gx", "gy"),
        P("gx", "gy"),
        P(("gx", "gy"), None, None),
        P(("gx", "gy"), None),
        P(("gx", "gy"), None),
        P(("gx", "gy"), None, None, None),
    )
    return jax.shard_map(
        functools.partial(body, gx_count=mesh.shape["gx"], gy_count=mesh.shape["gy"]),
        mesh=mesh,
        in_specs=placed,
        out_specs=(P(None, "gx", "gy"), P(("gx", "gy"), None), P("gx", "gy")),
        check_vma=False,
    )
```

```python
import functools
import math

import jax
import jax.numpy as jnp
from jax import lax
from jax.experimental import pallas as pl
from jax.experimental.pallas import tpu as pltpu
from jax.sharding import PartitionSpec as P

SWEEPS = 8
RESIDUAL = 0.05
SIDES = 4
PARTS = 2
BOTH = ("gx", "gy")
ORDER = ((0, 1), (1, 1), (0, 0), (1, 0))
F32 = jnp.float32
BF16 = jnp.bfloat16


def partner_of(index, count, odd):
    other = ((index - odd) ^ 1) + odd
    return other, 0 <= index - odd and 0 <= other < count


def swaps(gx_count, gy_count):
    perms = []
    for axis, odd in ORDER:
        perm = []
        for x in range(gx_count):
            for y in range(gy_count):
                if axis == 1:
                    other, fits = partner_of(y, gy_count, odd)
                    across = gy_count - 1 - y if gy_count % 2 == 0 else y
                    target = (x, other if fits else across)
                else:
                    other, fits = partner_of(x, gx_count, odd)
                    beside = y ^ 1 if gy_count % 2 == 0 and gx_count % 2 == 0 else y
                    target = (other, y) if fits else (x, beside)
                perm.append((x * gy_count + y, target[0] * gy_count + target[1]))
        perms.append(perm)
    return perms


def owners_here(gx_count, gy_count):
    x = lax.axis_index("gx")
    y = lax.axis_index("gy")

    def neighbour(index, count, odd, make):
        other = ((index - odd) ^ 1) + odd
        fits = (index >= odd) & (other < count)
        return jnp.where(fits, make(other), -1)

    along = lambda other: x * gy_count + other
    across = lambda other: other * gy_count + y
    found = [x * gy_count + y]
    for axis, odd in ORDER:
        found.append(neighbour(y, gy_count, odd, along) if axis else neighbour(x, gx_count, odd, across))
    return found


def soil_tile(place, water_ref, porosity_ref, conduct_ref, exponent_ref, inflow_ref):
    layers = water_ref.shape[0]
    power = exponent_ref[place]
    less = power - 1.0
    inverse = 1.0 / power
    kappa = jnp.exp2(
        (jnp.log2(power * conduct_ref[place]) - power * jnp.log2(porosity_ref[place] - RESIDUAL)) / less
    )
    back = 1.0 / kappa
    bend = less * (0.5 * math.log(2.0))
    inflow = inflow_ref[place] * (kappa * power)

    def layer(flux, content):
        turn = jnp.tanh(bend * jnp.log2(content))
        below = (flux + content) * (0.5 + 0.5 * turn)
        return below, content + (flux - below) * inverse

    pair = 2
    total = None
    for first in range(0, SWEEPS, pair):
        fluxes = [inflow] * pair
        contents = [None] * layers
        for diagonal in range(layers + pair - 1):
            for sweep in reversed(range(pair)):
                at = diagonal - sweep
                if not 0 <= at < layers:
                    continue
                here = (at,) + place
                if sweep:
                    content = contents[at]
                elif first:
                    content = water_ref[here]
                else:
                    content = (water_ref[here] - RESIDUAL) * kappa
                fluxes[sweep], content = layer(fluxes[sweep], content)
                contents[at] = content
                if sweep == pair - 1:
                    last = first + pair == SWEEPS
                    water_ref[here] = content * back + RESIDUAL if last else content
        for flux in fluxes:
            total = flux if total is None else total + flux
    return total * (back * inverse)


def bin_rows(target, value, keys, totals_ref):
    width = totals_ref.shape[1]
    rows, columns = target.shape
    slots_high = keys.shape[0]
    shift = width.bit_length() - 1
    keys = jnp.concatenate([keys] * (columns // 128), axis=1)
    cell = lax.broadcasted_iota(jnp.int32, (width, columns), 0).astype(F32).astype(BF16)
    cells = (target & (width - 1)).astype(F32)
    slot = lax.shift_right_logical(target, shift)
    high = value.astype(BF16).astype(F32)
    low = value - high
    one_hot = []
    spread = []
    for row in range(rows):
        line = slice(row, row + 1)
        wide = jnp.broadcast_to(cells[line], (16, columns)).astype(BF16)
        wide = jnp.concatenate([wide] * (width // 16), axis=0)
        one_hot.append(jnp.where(wide == cell, BF16(1), BF16(0)))
        hit = jnp.broadcast_to(slot[line], (slots_high, columns)) == keys
        parts = [
            jnp.where(hit, jnp.broadcast_to(part[line], (slots_high, columns)), 0.0) for part in (high, low)
        ]
        spread.append(jnp.concatenate(parts, axis=0).astype(BF16))
    totals_ref[...] += lax.dot_general(
        jnp.concatenate(spread, axis=1),
        jnp.concatenate(one_hot, axis=1),
        (((1,), (1,)), ((), ())),
        preferred_element_type=F32,
    )


def prepare(
    gx_count, gy_count, send, pattern, own_blocks, source_ref, block_ref, key_ref, part_key_ref, part_width
):
    hi_rows, width = key_ref.shape
    slots, devices = send.shape
    owners = owners_here(gx_count, gy_count)
    row = lax.broadcasted_iota(jnp.int32, (hi_rows, width), 0)
    keys = jnp.full((hi_rows, width), -1, jnp.int32)
    for k, owner in enumerate(owners):
        inside = (row >= k * slots) & (row < (k + 1) * slots) & (owner >= 0)
        keys = jnp.where(inside, owner * slots + row - k * slots, keys)
    key_ref[...] = keys
    parts = width // part_width
    entries = (SIDES + 1) * slots
    row = lax.broadcasted_iota(jnp.int32, part_key_ref.shape, 0)
    keys = jnp.full(part_key_ref.shape, -1, jnp.int32)
    for part in range(parts):
        for k, owner in enumerate(owners):
            first = part * entries + k * slots
            inside = (row >= first) & (row < first + slots) & (owner >= 0)
            keys = jnp.where(inside, (owner * slots + row - first) * parts + part, keys)
    part_key_ref[...] = keys
    lane = lax.broadcasted_iota(jnp.int32, (slots, devices), 1)
    block_ref[...] = jnp.full(block_ref.shape, -1, jnp.int32)
    for k, owner in enumerate(owners):
        idents = jnp.sum(jnp.where(lane == owner, send, 0), axis=1, keepdims=True)
        block_ref[k, 0:slots, :] = jnp.broadcast_to(idents, (slots, width))
    shift = own_blocks.bit_length() - 1
    most = pattern.shape[1]
    for k in range(most):
        ident = jnp.broadcast_to(pattern[:, k : k + 1], (own_blocks, width))
        side = jnp.full((own_blocks, width), -1, jnp.int32)
        for at, owner in enumerate(owners):
            side = jnp.where((lax.shift_right_arithmetic(ident, shift) == owner) & (ident >= 0), at, side)
        source_ref[k] = side
        source_ref[most + k] = ident & (own_blocks - 1)


def soil_kernel(
    gx_count, gy_count,
    water_hbm, porosity_hbm, conduct_hbm, exponent_hbm, inflow_hbm, target_hbm, heads_hbm,
    send_hbm, pattern_hbm, blocks_hbm,
    soil_hbm, source_ref, block_ref, key_ref, own_ref, *rest,
):
    side_refs = rest[:SIDES]
    (
        blocks_out, water_ref, porosity_ref, conduct_ref, exponent_ref, inflow_ref, target_ref,
        heads_ref, send_ref, pattern_ref, recharge_ref, part_key_ref, totals_ref, small_sems, in_sems, out_sems, blocks_sem,
    ) = rest[SIDES:]
    rows, columns = target_ref.shape
    own_blocks, width = heads_ref.shape
    slots = send_ref.shape[0]
    chunks = in_sems.shape[0]
    chunk = rows // chunks
    flats = (
        (porosity_hbm, porosity_ref), (conduct_hbm, conduct_ref), (exponent_hbm, exponent_ref),
        (inflow_hbm, inflow_ref), (target_hbm, target_ref),
    )

    def small_copies():
        pairs = ((send_hbm, send_ref), (pattern_hbm, pattern_ref), (heads_hbm, heads_ref))
        return [pltpu.make_async_copy(a, b, small_sems.at[at]) for at, (a, b) in enumerate(pairs)]

    def incoming(at):
        here = (pl.ds(pl.multiple_of(at * chunk, 8), chunk), slice(None))
        deep = (slice(None),) + here
        copies = [pltpu.make_async_copy(a.at[here], b.at[here], in_sems.at[at, f]) for f, (a, b) in enumerate(flats)]
        return copies + [pltpu.make_async_copy(water_hbm.at[deep], water_ref.at[deep], in_sems.at[at, len(flats)])]

    def outgoing(at):
        deep = (slice(None), pl.ds(pl.multiple_of(at * chunk, 8), chunk), slice(None))
        return pltpu.make_async_copy(water_ref.at[deep], soil_hbm.at[deep], out_sems.at[at])

    blocks_copy = pltpu.make_async_copy(blocks_hbm, blocks_out, blocks_sem)
    for copy in small_copies() + incoming(0) + incoming(1):
        copy.start()
    totals_ref[...] = jnp.zeros_like(totals_ref)
    recharge_ref[0:8, :] = jnp.zeros((8, columns), F32)
    for copy in small_copies():
        copy.wait()
    prepare(
        gx_count, gy_count, send_ref[...], pattern_ref[...], own_blocks, source_ref, block_ref, key_ref,
        part_key_ref, totals_ref.shape[1],
    )

    def bin_tile(tile):
        target = target_ref[pl.ds(pl.multiple_of(jnp.maximum(tile, 0) * 8, 8), 8), :]
        value = recharge_ref[pl.ds(pl.multiple_of(tile * 8 + 8, 8), 8), :]
        bin_rows(target, value, part_key_ref[...], totals_ref)

    @pl.loop(0, chunks)
    def _(at):
        for copy in incoming(at):
            copy.wait()

        @pl.when(at + 2 < chunks)
        def _():
            for copy in incoming(at + 2):
                copy.start()

        @pl.when(at == chunks - 2)
        def _():
            blocks_copy.start()

        for tile in range(chunk // 8):
            tile = at * (chunk // 8) + tile
            bin_tile(tile - 1)
            place = (pl.ds(pl.multiple_of(tile * 8, 8), 8), slice(None))
            recharge_ref[pl.ds(pl.multiple_of(tile * 8 + 8, 8), 8), :] = soil_tile(
                place, water_ref, porosity_ref, conduct_ref, exponent_ref, inflow_ref
            )

        outgoing(at).start()

    bin_tile(rows // 8 - 1)
    part_rows = part_key_ref.shape[0]
    entries = (SIDES + 1) * slots
    sums = totals_ref[0:part_rows, :] + totals_ref[part_rows : 2 * part_rows, :]
    parts = width // totals_ref.shape[1]
    sums = jnp.concatenate([sums[part * entries : (part + 1) * entries] for part in range(parts)], axis=1)
    block = lax.broadcasted_iota(jnp.int32, (own_blocks, width), 0)
    for k in range(SIDES + 1):
        out_ref = side_refs[k - 1] if k else own_ref
        idents = block_ref[k]
        placed = jnp.zeros((own_blocks, width), F32)
        for slot in range(slots):
            at = k * slots + slot
            placed = placed + jnp.where(block == idents[slot : slot + 1], sums[at : at + 1], 0.0)
        out_ref[0:own_blocks, :] = placed
        out_ref[own_blocks : 2 * own_blocks, :] = heads_ref[...]
    blocks_copy.wait()

    @pl.loop(0, chunks)
    def _(at):
        outgoing(at).wait()


def operate(source_ref, blocks_ref, fields):
    own_blocks, most, width = blocks_ref.shape[:3]
    nearby = []
    for k in range(most):
        side, line = source_ref[k], source_ref[most + k]
        rows = jnp.zeros((own_blocks, width), F32)
        for at, field in enumerate(fields):
            picked = jnp.take_along_axis(field, line, axis=0, mode="promise_in_bounds")
            rows = jnp.where(side == at, picked, rows)
        nearby.append(rows)
    image = jnp.zeros((own_blocks, width), F32)
    row = lax.broadcasted_iota(jnp.int32, (own_blocks, 3 * width), 0)
    for r in range(own_blocks):
        total = blocks_ref[r, 0] * nearby[0][r : r + 1]
        for k in range(1, most):
            total = total + blocks_ref[r, k] * nearby[k][r : r + 1]
        first = total.astype(BF16)
        rest = total - first.astype(F32)
        second = rest.astype(BF16)
        third = (rest - second.astype(F32)).astype(BF16)
        parts = jnp.concatenate([first, second, third], axis=1)
        ones = jnp.where(row == r, 1.0, 0.0).astype(BF16)
        image = image + lax.dot_general(
            ones, parts, (((1,), (1,)), ((), ())), preferred_element_type=F32
        )
    return image


def start_kernel(area, source_ref, blocks_ref, own_ref, *rest):
    side_refs, residual_ref = rest[:SIDES], rest[SIDES]
    own_blocks = residual_ref.shape[0]
    heads = own_ref[own_blocks:, :]
    cells = own_ref[:own_blocks, :]
    for side in side_refs:
        cells = cells + side[:own_blocks, :]
    fields = [heads] + [s[own_blocks:, :] for s in side_refs]
    residual_ref[...] = heads + area * cells - operate(source_ref, blocks_ref, fields)


def apply_kernel(source_ref, blocks_ref, *rest):
    image_ref = rest[-1]
    fields = [f[...] for f in (rest[0],) + rest[-2:0:-1]]
    image_ref[...] = operate(source_ref, blocks_ref, fields)


def whole_sum(values):
    return jnp.sum(jnp.sum(values, axis=0, keepdims=True), axis=1, keepdims=True)


def last_kernel(source_ref, blocks_ref, r_ref, w_ref, *rest):
    fields, sums_ref = [f[...] for f in (rest[0],) + rest[-2:0:-1]], rest[-1]
    z = operate(source_ref, blocks_ref, fields)
    r, w, v = r_ref[...], w_ref[...], fields[0]
    rr = whole_sum(r * r)
    ratio = whole_sum(w * w) / rr
    shift = jnp.where((ratio > 0.0) & (ratio < 1e30), jnp.sqrt(ratio), 1.0)
    inverse = 1.0 / shift
    w1 = w * inverse - r
    v1 = (v * inverse - w) * inverse
    z1 = ((z * inverse - v) * inverse) * inverse
    v2 = v1 - w1
    z2 = z1 - v1
    z3 = z2 - v2
    sums = [
        rr, shift,
        whole_sum(r * w1), whole_sum(w1 * w1), whole_sum(r * v2), whole_sum(w1 * v2), whole_sum(v2 * v2),
        whole_sum(r * z3), whole_sum(w1 * z3), whole_sum(v2 * z3),
    ]
    lane = lax.broadcasted_iota(jnp.int32, (1, 128), 1)
    packed = jnp.zeros((1, 128), F32)
    for position, value in enumerate(sums):
        packed = jnp.where(lane == position, value, packed)
    sums_ref[...] = jnp.broadcast_to(packed[None], sums_ref.shape)


def solve_step(all_sums):
    lane = lax.broadcasted_iota(jnp.int32, all_sums.shape, 1)

    def take(position):
        return jnp.sum(jnp.where(lane == position, all_sums, 0.0), axis=1, keepdims=True)

    rr, shift, rw, ww, rv, wv, vv, rz, wz, vz = [take(p) for p in range(10)]

    def over(values):
        return jnp.sum(values, axis=0, keepdims=True)

    m0 = over(rr)
    theta = over(shift * (rw + rr)) / m0
    ratio = shift / theta
    e = ratio - 1.0
    p2 = ratio * ratio
    p3 = p2 * ratio
    p4 = p2 * p2
    rw, ww, rv = rw * ratio, ww * p2, rv * p2
    wv, rz = wv * p3, rz * p3
    vv, wz = vv * p4, wz * p4
    vz = vz * (p4 * ratio)
    e2 = e * e
    twice = 2.0 * e
    new_w_r = rw + e * rr
    new_w_w = ww + e * rw
    new_v_r = rv + twice * rw + e2 * rr
    new_v_w = wv + twice * ww + e2 * rw
    new_v_v = vv + twice * wv + e2 * rv
    m1 = over(new_w_r)
    m2 = over(new_w_w + e * new_w_r)
    m3 = over(wv + e * rv + twice * new_w_w + e2 * new_w_r)
    m4 = over(new_v_v + twice * new_v_w + e2 * new_v_r)
    m5 = over(vz + twice * wz + e2 * rz + 3.0 * e * new_v_v + 3.0 * e2 * new_v_w + e * e2 * new_v_r)
    a00, a01, a02 = m0 + m1, m1 + m2, m2 + m3
    a11, a12, a22 = m2 + m3, m3 + m4, m4 + m5
    f1 = a01 / a00
    f2 = a02 / a00
    b11 = a11 - f1 * a01
    b12 = a12 - f1 * a02
    b22 = a22 - f2 * a02
    g1 = m1 - f1 * m0
    g2 = m2 - f2 * m0
    f3 = b12 / b11
    y2 = (g2 - f3 * g1) / (b22 - f3 * b12)
    y1 = (g1 - b12 * y2) / b11
    y0 = (m0 - a01 * y1 - a02 * y2) / a00
    inverse = 1.0 / theta
    y2 = y2 * inverse
    return (y0 - y1) * inverse + y2, (y1 * inverse - 2.0 * y2) * inverse, y2 * inverse * inverse


def heads_kernel(slots, block_ref, key_ref, all_ref, target_ref, own_ref, r_ref, w_ref, v_ref, *rest):
    sides = rest[: 4 * SIDES]
    heads_hbm, columns_hbm, slot_ref, heads_ref, columns_ref, sems = rest[4 * SIDES :]
    own_blocks, width = r_ref.shape
    shift = width.bit_length() - 1
    weight_r, weight_w, weight_v = solve_step(all_ref[:, 0, :])

    def new_heads(old, r, w, v):
        return old[own_blocks:, :] + weight_r * r[...] + weight_w * w[...] + weight_v * v[...]

    heads_copy = pltpu.make_async_copy(heads_ref, heads_hbm, sems.at[0])
    for k in range(SIDES + 1):
        four = sides[4 * k - 4 : 4 * k] if k else (own_ref, r_ref, w_ref, v_ref)
        heads = new_heads(*four)
        if k == 0:
            heads_ref[...] = heads
            heads_copy.start()
        lines = jnp.maximum(block_ref[k], 0)
        picked = jnp.take_along_axis(heads, lines, axis=0, mode="promise_in_bounds")
        for slot in range(slots):
            slot_ref[k * slots + slot] = jnp.broadcast_to(picked[slot : slot + 1], (8, width))
    entries = (SIDES + 1) * slots
    rows, columns = target_ref.shape
    copies = []
    for at in range(0, rows, 8):
        for part in range(0, columns, 128):
            here = (slice(at, at + 8), slice(part, part + 128))
            target = target_ref[here]
            lanes = target & (width - 1)
            key = lax.shift_right_logical(target, shift)
            found = jnp.zeros((8, 128), F32)
            for entry in range(entries):
                values = jnp.take_along_axis(slot_ref[entry], lanes, axis=1, mode="promise_in_bounds")
                wanted = jnp.broadcast_to(key_ref[entry : entry + 1, :], (8, 128))
                found = jnp.where(key == wanted, values, found)
            columns_ref[here] = found
        if (at + 8) % 16 == 0:
            here = (slice(at - 8, at + 8), slice(None))
            copies.append(
                pltpu.make_async_copy(columns_ref.at[here], columns_hbm.at[here], sems.at[1 + len(copies)])
            )
            copies[-1].start()
    heads_copy.wait()
    for copy in copies:
        copy.wait()


VMEM = pl.BlockSpec(memory_space=pltpu.VMEM)
ANY = pl.BlockSpec(memory_space=pl.ANY)


def body(
    water_content,
    porosity,
    conduct,
    exponent,
    infiltration,
    column_target,
    send_blocks,
    prior_heads,
    block_pattern,
    aquifer_blocks,
    gx_count,
    gy_count,
):
    devices, slots = send_blocks.shape[1:]
    own_blocks, width = prior_heads.shape
    layers, rows, columns = water_content.shape
    most = block_pattern.shape[1]
    hi_rows = -(-(SIDES + 1) * slots // 8) * 8
    part_rows = -(-PARTS * (SIDES + 1) * slots // 8) * 8
    area = own_blocks * width / (rows * columns)
    perms = swaps(gx_count, gy_count)
    in_hbm = lambda array: pltpu.with_memory_space_constraint(array, pltpu.HBM)
    field = jax.ShapeDtypeStruct((own_blocks, width), F32)
    two = jax.ShapeDtypeStruct((2 * own_blocks, width), F32)

    def trade(array):
        return [lax.ppermute(array, BOTH, perm) for perm in perms]

    chunks = rows // 16
    outs = pl.pallas_call(
        functools.partial(soil_kernel, gx_count, gy_count),
        in_specs=[ANY] * 10,
        out_specs=[ANY] + [VMEM] * (SIDES + 4) + [ANY],
        out_shape=[
            jax.ShapeDtypeStruct(water_content.shape, F32),
            jax.ShapeDtypeStruct((2 * most, own_blocks, width), jnp.int32),
            jax.ShapeDtypeStruct((SIDES + 1, own_blocks, width), jnp.int32),
            jax.ShapeDtypeStruct((hi_rows, width), jnp.int32),
        ]
        + [two] * (SIDES + 1)
        + [pltpu.VMEM(aquifer_blocks.shape, F32)],
        scratch_shapes=[
            pltpu.VMEM(water_content.shape, F32),
            *[pltpu.VMEM((rows, columns), F32)] * 4,
            pltpu.VMEM((rows, columns), jnp.int32),
            pltpu.VMEM((own_blocks, width), F32),
            pltpu.VMEM((slots, devices), jnp.int32),
            pltpu.VMEM((own_blocks, most), jnp.int32),
            pltpu.VMEM((rows + 8, columns), F32),
            pltpu.VMEM((part_rows, width), jnp.int32),
            pltpu.VMEM((2 * part_rows, width // PARTS), F32),
            pltpu.SemaphoreType.DMA((3,)),
            pltpu.SemaphoreType.DMA((chunks, 6)),
            pltpu.SemaphoreType.DMA((chunks,)),
            pltpu.SemaphoreType.DMA,
        ],
        compiler_params=pltpu.CompilerParams(vmem_limit_bytes=24 * 2**20),
        name="soil",
    )(
        *map(
            in_hbm,
            (
                water_content, porosity, conduct, exponent, infiltration, column_target, prior_heads,
                send_blocks[0].T, block_pattern, aquifer_blocks,
            ),
        )
    )
    soil_water, source, block, key, own = outs[:5]
    blocks = pltpu.with_memory_space_constraint(outs[-1], pltpu.VMEM)
    got = [lax.ppermute(out, BOTH, perm) for out, perm in zip(outs[5:], perms)]

    def small(kernel, args, shape, name):
        return pl.pallas_call(
            kernel,
            in_specs=[VMEM] * (2 + len(args)),
            out_specs=VMEM,
            out_shape=shape,
            compiler_params=pltpu.CompilerParams(vmem_limit_bytes=16 * 2**20),
            name=name,
        )(source, blocks, *args)

    r = small(functools.partial(start_kernel, area), (own, *got), field, "start")
    r_sides = trade(r)
    w = small(apply_kernel, (r, *r_sides[::-1]), field, "once")
    w_sides = trade(w)
    v = small(apply_kernel, (w, *w_sides[::-1]), field, "twice")
    v_sides = trade(v)
    sums = small(last_kernel, (r, w, v, *v_sides[::-1]), jax.ShapeDtypeStruct((devices, 1, width), F32), "sums")
    all_sums = lax.all_to_all(sums, BOTH, 0, 0)
    sides = []
    for k in range(SIDES):
        sides += [got[k], r_sides[k], w_sides[k], v_sides[k]]
    heads, column_heads = pl.pallas_call(
        functools.partial(heads_kernel, slots),
        in_specs=[VMEM] * (8 + 4 * SIDES),
        out_specs=[ANY, ANY],
        out_shape=[field, jax.ShapeDtypeStruct((rows, columns), F32)],
        scratch_shapes=[
            pltpu.VMEM((hi_rows, 8, width), F32),
            pltpu.VMEM((own_blocks, width), F32),
            pltpu.VMEM((rows, columns), F32),
            pltpu.SemaphoreType.DMA((1 + rows // 16,)),
        ],
        compiler_params=pltpu.CompilerParams(vmem_limit_bytes=16 * 2**20),
        name="heads",
    )(block, key, all_sums, column_target, own, r, w, v, *sides)
    return soil_water, heads, column_heads


def solution(mesh):
    placed = (
        P(None, "gx", "gy"),
        P("gx", "gy"),
        P("gx", "gy"),
        P("gx", "gy"),
        P("gx", "gy"),
        P("gx", "gy"),
        P(("gx", "gy"), None, None),
        P(("gx", "gy"), None),
        P(("gx", "gy"), None),
        P(("gx", "gy"), None, None, None),
    )
    return jax.shard_map(
        functools.partial(body, gx_count=mesh.shape["gx"], gy_count=mesh.shape["gy"]),
        mesh=mesh,
        in_specs=placed,
        out_specs=(P(None, "gx", "gy"), P(("gx", "gy"), None), P("gx", "gy")),
        check_vma=False,
    )
```

```python
import functools
import math

import jax
import jax.numpy as jnp
from jax import lax
from jax.experimental import pallas as pl
from jax.experimental.pallas import tpu as pltpu
from jax.sharding import PartitionSpec as P

SWEEPS = 8
RESIDUAL = 0.05
SIDES = 4
PARTS = 2
BOTH = ("gx", "gy")
ORDER = ((0, 1), (1, 1), (0, 0), (1, 0))
F32 = jnp.float32
BF16 = jnp.bfloat16


def partner_of(index, count, odd):
    other = ((index - odd) ^ 1) + odd
    return other, 0 <= index - odd and 0 <= other < count


def swaps(gx_count, gy_count):
    perms = []
    for axis, odd in ORDER:
        perm = []
        for x in range(gx_count):
            for y in range(gy_count):
                if axis == 1:
                    other, fits = partner_of(y, gy_count, odd)
                    across = gy_count - 1 - y if gy_count % 2 == 0 else y
                    target = (x, other if fits else across)
                else:
                    other, fits = partner_of(x, gx_count, odd)
                    beside = y ^ 1 if gy_count % 2 == 0 and gx_count % 2 == 0 else y
                    target = (other, y) if fits else (x, beside)
                perm.append((x * gy_count + y, target[0] * gy_count + target[1]))
        perms.append(perm)
    return perms


def owners_here(gx_count, gy_count):
    x = lax.axis_index("gx")
    y = lax.axis_index("gy")

    def neighbour(index, count, odd, make):
        other = ((index - odd) ^ 1) + odd
        fits = (index >= odd) & (other < count)
        return jnp.where(fits, make(other), -1)

    along = lambda other: x * gy_count + other
    across = lambda other: other * gy_count + y
    found = [x * gy_count + y]
    for axis, odd in ORDER:
        found.append(neighbour(y, gy_count, odd, along) if axis else neighbour(x, gx_count, odd, across))
    return found


def soil_tile(place, water_ref, porosity_ref, conduct_ref, exponent_ref, inflow_ref):
    layers = water_ref.shape[0]
    power = exponent_ref[place]
    less = power - 1.0
    inverse = 1.0 / power
    kappa = jnp.exp2(
        (jnp.log2(power * conduct_ref[place]) - power * jnp.log2(porosity_ref[place] - RESIDUAL)) / less
    )
    back = 1.0 / kappa
    bend = less * (0.5 * math.log(2.0))
    inflow = inflow_ref[place] * (kappa * power)

    def layer(flux, content):
        turn = jnp.tanh(bend * jnp.log2(content))
        below = (flux + content) * (0.5 + 0.5 * turn)
        return below, content + (flux - below) * inverse

    pair = 2
    total = None
    for first in range(0, SWEEPS, pair):
        fluxes = [inflow] * pair
        contents = [None] * layers
        for diagonal in range(layers + pair - 1):
            for sweep in reversed(range(pair)):
                at = diagonal - sweep
                if not 0 <= at < layers:
                    continue
                here = (at,) + place
                if sweep:
                    content = contents[at]
                elif first:
                    content = water_ref[here]
                else:
                    content = (water_ref[here] - RESIDUAL) * kappa
                fluxes[sweep], content = layer(fluxes[sweep], content)
                contents[at] = content
                if sweep == pair - 1:
                    last = first + pair == SWEEPS
                    water_ref[here] = content * back + RESIDUAL if last else content
        for flux in fluxes:
            total = flux if total is None else total + flux
    return total * (back * inverse)


def bin_rows(target, value, part, totals_ref):
    width = totals_ref.shape[1]
    part_rows = totals_ref.shape[0] // 2
    rows, columns = target.shape
    cell = lax.broadcasted_iota(jnp.int32, (width, columns), 0).astype(F32).astype(BF16)
    cells = (target & (width - 1)).astype(F32)
    part = part.astype(F32)
    keys = lax.broadcasted_iota(jnp.int32, (part_rows, columns), 0).astype(F32).astype(BF16)
    high = value.astype(BF16).astype(F32)
    low = value - high
    one_hot = []
    spread = []
    for row in range(rows):
        line = slice(row, row + 1)
        def wide(array, count):
            packed = jnp.broadcast_to(array[line], (16, columns)).astype(BF16)
            return jnp.concatenate([packed] * (count // 16), axis=0)

        one_hot.append(jnp.where(wide(cells, width) == cell, BF16(1), BF16(0)))
        hit = wide(part, part_rows) == keys
        parts = [jnp.where(hit, wide(piece, part_rows), BF16(0)) for piece in (high, low)]
        spread.append(jnp.concatenate(parts, axis=0))
    totals_ref[...] += lax.dot_general(
        jnp.concatenate(spread, axis=1),
        jnp.concatenate(one_hot, axis=1),
        (((1,), (1,)), ((), ())),
        preferred_element_type=F32,
    )


def prepare(gx_count, gy_count, send, pattern, own_blocks, source_ref, block_ref, key_ref):
    hi_rows, width = key_ref.shape
    slots, devices = send.shape
    owners = owners_here(gx_count, gy_count)
    row = lax.broadcasted_iota(jnp.int32, (hi_rows, width), 0)
    keys = jnp.full((hi_rows, width), -1, jnp.int32)
    for k, owner in enumerate(owners):
        inside = (row >= k * slots) & (row < (k + 1) * slots) & (owner >= 0)
        keys = jnp.where(inside, owner * slots + row - k * slots, keys)
    key_ref[...] = keys
    lane = lax.broadcasted_iota(jnp.int32, (slots, devices), 1)
    block_ref[...] = jnp.full(block_ref.shape, -1, jnp.int32)
    for k, owner in enumerate(owners):
        idents = jnp.sum(jnp.where(lane == owner, send, 0), axis=1, keepdims=True)
        block_ref[k, 0:slots, :] = jnp.broadcast_to(idents, (slots, width))
    shift = own_blocks.bit_length() - 1
    most = pattern.shape[1]
    for k in range(most):
        ident = jnp.broadcast_to(pattern[:, k : k + 1], (own_blocks, width))
        side = jnp.full((own_blocks, width), -1, jnp.int32)
        for at, owner in enumerate(owners):
            side = jnp.where((lax.shift_right_arithmetic(ident, shift) == owner) & (ident >= 0), at, side)
        source_ref[k] = side
        source_ref[most + k] = ident & (own_blocks - 1)


def soil_kernel(
    gx_count, gy_count,
    water_hbm, porosity_hbm, conduct_hbm, exponent_hbm, inflow_hbm, target_hbm, heads_hbm,
    send_hbm, pattern_hbm, blocks_hbm,
    soil_hbm, source_ref, block_ref, key_ref, own_ref, *rest,
):
    side_refs = rest[:SIDES]
    (
        blocks_out, water_ref, porosity_ref, conduct_ref, exponent_ref, inflow_ref, target_ref,
        heads_ref, send_ref, pattern_ref, recharge_ref, totals_ref, small_sems, in_sems, out_sems, blocks_sem,
    ) = rest[SIDES:]
    rows, columns = target_ref.shape
    own_blocks, width = heads_ref.shape
    slots = send_ref.shape[0]
    chunks = in_sems.shape[0]
    chunk = rows // chunks
    flats = (
        (porosity_hbm, porosity_ref), (conduct_hbm, conduct_ref), (exponent_hbm, exponent_ref),
        (inflow_hbm, inflow_ref), (target_hbm, target_ref),
    )

    def small_copies():
        pairs = ((send_hbm, send_ref), (pattern_hbm, pattern_ref), (heads_hbm, heads_ref))
        return [pltpu.make_async_copy(a, b, small_sems.at[at]) for at, (a, b) in enumerate(pairs)]

    def incoming(at):
        here = (pl.ds(pl.multiple_of(at * chunk, 8), chunk), slice(None))
        deep = (slice(None),) + here
        copies = [pltpu.make_async_copy(a.at[here], b.at[here], in_sems.at[at, f]) for f, (a, b) in enumerate(flats)]
        return copies + [pltpu.make_async_copy(water_hbm.at[deep], water_ref.at[deep], in_sems.at[at, len(flats)])]

    def outgoing(at):
        deep = (slice(None), pl.ds(pl.multiple_of(at * chunk, 8), chunk), slice(None))
        return pltpu.make_async_copy(water_ref.at[deep], soil_hbm.at[deep], out_sems.at[at])

    blocks_copy = pltpu.make_async_copy(blocks_hbm, blocks_out, blocks_sem)
    for copy in small_copies() + incoming(0) + incoming(1):
        copy.start()
    totals_ref[...] = jnp.zeros_like(totals_ref)
    recharge_ref[0:chunk, :] = jnp.zeros((chunk, columns), F32)
    for copy in small_copies():
        copy.wait()
    prepare(
        gx_count, gy_count, send_ref[...], pattern_ref[...], own_blocks, source_ref, block_ref, key_ref
    )

    owners = owners_here(gx_count, gy_count)
    entries = (SIDES + 1) * slots
    shift = totals_ref.shape[1].bit_length() - 1
    parts = width // totals_ref.shape[1]

    def part_of(target):
        part = lax.shift_right_logical(target, shift)
        slot = lax.shift_right_logical(part, parts.bit_length() - 1)
        owner = lax.shift_right_logical(slot, slots.bit_length() - 1)
        side = jnp.zeros_like(target)
        for k in range(1, SIDES + 1):
            side = jnp.where(owner == owners[k], k * slots, side)
        return side + (slot & (slots - 1)) + (part & (parts - 1)) * entries

    def bin_chunk(at):
        target = target_ref[pl.ds(pl.multiple_of(jnp.maximum(at, 0) * chunk, 8), chunk), :]
        value = recharge_ref[pl.ds(pl.multiple_of(at * chunk + chunk, 8), chunk), :]
        bin_rows(target, value, part_of(target), totals_ref)

    @pl.loop(0, chunks)
    def _(at):
        for copy in incoming(at):
            copy.wait()

        @pl.when(at + 2 < chunks)
        def _():
            for copy in incoming(at + 2):
                copy.start()

        @pl.when(at == chunks - 2)
        def _():
            blocks_copy.start()

        bin_chunk(at - 1)
        for tile in range(chunk // 8):
            tile = at * (chunk // 8) + tile
            place = (pl.ds(pl.multiple_of(tile * 8, 8), 8), slice(None))
            recharge_ref[pl.ds(pl.multiple_of(tile * 8 + chunk, 8), 8), :] = soil_tile(
                place, water_ref, porosity_ref, conduct_ref, exponent_ref, inflow_ref
            )

        outgoing(at).start()

    bin_chunk(chunks - 1)
    part_rows = totals_ref.shape[0] // 2
    sums = totals_ref[0:part_rows, :] + totals_ref[part_rows : 2 * part_rows, :]
    sums = jnp.concatenate([sums[part * entries : (part + 1) * entries] for part in range(parts)], axis=1)
    block = lax.broadcasted_iota(jnp.int32, (own_blocks, width), 0)
    for k in range(SIDES + 1):
        out_ref = side_refs[k - 1] if k else own_ref
        idents = block_ref[k]
        placed = jnp.zeros((own_blocks, width), F32)
        for slot in range(slots):
            at = k * slots + slot
            placed = placed + jnp.where(block == idents[slot : slot + 1], sums[at : at + 1], 0.0)
        out_ref[0:own_blocks, :] = placed
        out_ref[own_blocks : 2 * own_blocks, :] = heads_ref[...]
    blocks_copy.wait()

    @pl.loop(0, chunks)
    def _(at):
        outgoing(at).wait()


def operate(source_ref, blocks_ref, fields, pieces=3):
    own_blocks, most, width = blocks_ref.shape[:3]
    nearby = []
    for k in range(most):
        side, line = source_ref[k], source_ref[most + k]
        rows = jnp.zeros((own_blocks, width), F32)
        for at, field in enumerate(fields):
            picked = jnp.take_along_axis(field, line, axis=0, mode="promise_in_bounds")
            rows = jnp.where(side == at, picked, rows)
        nearby.append(rows)
    image = jnp.zeros((own_blocks, width), F32)
    row = lax.broadcasted_iota(jnp.int32, (own_blocks, pieces * width), 0)
    for r in range(own_blocks):
        total = blocks_ref[r, 0] * nearby[0][r : r + 1]
        for k in range(1, most):
            total = total + blocks_ref[r, k] * nearby[k][r : r + 1]
        first = total.astype(BF16)
        rest = total - first.astype(F32)
        second = rest.astype(BF16)
        parts = [first, second]
        if pieces == 3:
            parts.append((rest - second.astype(F32)).astype(BF16))
        parts = jnp.concatenate(parts, axis=1)
        ones = jnp.where(row == r, 1.0, 0.0).astype(BF16)
        image = image + lax.dot_general(
            ones, parts, (((1,), (1,)), ((), ())), preferred_element_type=F32
        )
    return image


def start_kernel(area, source_ref, blocks_ref, own_ref, *rest):
    side_refs, residual_ref = rest[:SIDES], rest[SIDES]
    own_blocks = residual_ref.shape[0]
    heads = own_ref[own_blocks:, :]
    cells = own_ref[:own_blocks, :]
    for side in side_refs:
        cells = cells + side[:own_blocks, :]
    fields = [heads] + [s[own_blocks:, :] for s in side_refs]
    residual_ref[...] = heads + area * cells - operate(source_ref, blocks_ref, fields)


def apply_kernel(source_ref, blocks_ref, *rest):
    image_ref = rest[-1]
    fields = [f[...] for f in (rest[0],) + rest[-2:0:-1]]
    image_ref[...] = operate(source_ref, blocks_ref, fields)


def whole_sum(values):
    return jnp.sum(jnp.sum(values, axis=0, keepdims=True), axis=1, keepdims=True)


def last_kernel(source_ref, blocks_ref, r_ref, w_ref, *rest):
    fields, sums_ref = [f[...] for f in (rest[0],) + rest[-2:0:-1]], rest[-1]
    z = operate(source_ref, blocks_ref, fields, 2)
    r, w, v = r_ref[...], w_ref[...], fields[0]
    rr = whole_sum(r * r)
    ratio = whole_sum(w * w) / rr
    shift = jnp.where((ratio > 0.0) & (ratio < 1e30), jnp.sqrt(ratio), 1.0)
    inverse = 1.0 / shift
    w1 = w * inverse - r
    v1 = (v * inverse - w) * inverse
    z1 = ((z * inverse - v) * inverse) * inverse
    v2 = v1 - w1
    z2 = z1 - v1
    z3 = z2 - v2
    sums = [
        rr, shift,
        whole_sum(r * w1), whole_sum(w1 * w1), whole_sum(r * v2), whole_sum(w1 * v2), whole_sum(v2 * v2),
        whole_sum(r * z3), whole_sum(w1 * z3), whole_sum(v2 * z3),
    ]
    lane = lax.broadcasted_iota(jnp.int32, (1, 128), 1)
    packed = jnp.zeros((1, 128), F32)
    for position, value in enumerate(sums):
        packed = jnp.where(lane == position, value, packed)
    sums_ref[...] = jnp.broadcast_to(packed[None], sums_ref.shape)


def solve_step(all_sums):
    lane = lax.broadcasted_iota(jnp.int32, all_sums.shape, 1)

    def take(position):
        return jnp.sum(jnp.where(lane == position, all_sums, 0.0), axis=1, keepdims=True)

    rr, shift, rw, ww, rv, wv, vv, rz, wz, vz = [take(p) for p in range(10)]

    def over(values):
        return jnp.sum(values, axis=0, keepdims=True)

    m0 = over(rr)
    theta = over(shift * (rw + rr)) / m0
    ratio = shift / theta
    e = ratio - 1.0
    p2 = ratio * ratio
    p3 = p2 * ratio
    p4 = p2 * p2
    rw, ww, rv = rw * ratio, ww * p2, rv * p2
    wv, rz = wv * p3, rz * p3
    vv, wz = vv * p4, wz * p4
    vz = vz * (p4 * ratio)
    e2 = e * e
    twice = 2.0 * e
    new_w_r = rw + e * rr
    new_w_w = ww + e * rw
    new_v_r = rv + twice * rw + e2 * rr
    new_v_w = wv + twice * ww + e2 * rw
    new_v_v = vv + twice * wv + e2 * rv
    m1 = over(new_w_r)
    m2 = over(new_w_w + e * new_w_r)
    m3 = over(wv + e * rv + twice * new_w_w + e2 * new_w_r)
    m4 = over(new_v_v + twice * new_v_w + e2 * new_v_r)
    m5 = over(vz + twice * wz + e2 * rz + 3.0 * e * new_v_v + 3.0 * e2 * new_v_w + e * e2 * new_v_r)
    a00, a01, a02 = m0 + m1, m1 + m2, m2 + m3
    a11, a12, a22 = m2 + m3, m3 + m4, m4 + m5
    f1 = a01 / a00
    f2 = a02 / a00
    b11 = a11 - f1 * a01
    b12 = a12 - f1 * a02
    b22 = a22 - f2 * a02
    g1 = m1 - f1 * m0
    g2 = m2 - f2 * m0
    f3 = b12 / b11
    y2 = (g2 - f3 * g1) / (b22 - f3 * b12)
    y1 = (g1 - b12 * y2) / b11
    y0 = (m0 - a01 * y1 - a02 * y2) / a00
    inverse = 1.0 / theta
    y2 = y2 * inverse
    return (y0 - y1) * inverse + y2, (y1 * inverse - 2.0 * y2) * inverse, y2 * inverse * inverse


def heads_kernel(slots, block_ref, key_ref, all_ref, target_ref, own_ref, r_ref, w_ref, v_ref, *rest):
    sides = rest[: 4 * SIDES]
    heads_hbm, columns_hbm, slot_ref, heads_ref, columns_ref, sems = rest[4 * SIDES :]
    own_blocks, width = r_ref.shape
    shift = width.bit_length() - 1
    weight_r, weight_w, weight_v = solve_step(all_ref[:, 0, :])

    def new_heads(old, r, w, v):
        return old[own_blocks:, :] + weight_r * r[...] + weight_w * w[...] + weight_v * v[...]

    heads_copy = pltpu.make_async_copy(heads_ref, heads_hbm, sems.at[0])
    for k in range(SIDES + 1):
        four = sides[4 * k - 4 : 4 * k] if k else (own_ref, r_ref, w_ref, v_ref)
        heads = new_heads(*four)
        if k == 0:
            heads_ref[...] = heads
            heads_copy.start()
        lines = jnp.maximum(block_ref[k], 0)
        picked = jnp.take_along_axis(heads, lines, axis=0, mode="promise_in_bounds")
        for slot in range(slots):
            slot_ref[k * slots + slot] = jnp.broadcast_to(picked[slot : slot + 1], (8, width))
    entries = (SIDES + 1) * slots
    rows, columns = target_ref.shape
    copies = []
    for at in range(0, rows, 8):
        for part in range(0, columns, 128):
            here = (slice(at, at + 8), slice(part, part + 128))
            target = target_ref[here]
            lanes = target & (width - 1)
            key = lax.shift_right_logical(target, shift)
            found = jnp.zeros((8, 128), F32)
            for entry in range(entries):
                values = jnp.take_along_axis(slot_ref[entry], lanes, axis=1, mode="promise_in_bounds")
                wanted = jnp.broadcast_to(key_ref[entry : entry + 1, :], (8, 128))
                found = jnp.where(key == wanted, values, found)
            columns_ref[here] = found
        if (at + 8) % 16 == 0:
            here = (slice(at - 8, at + 8), slice(None))
            copies.append(
                pltpu.make_async_copy(columns_ref.at[here], columns_hbm.at[here], sems.at[1 + len(copies)])
            )
            copies[-1].start()
    heads_copy.wait()
    for copy in copies:
        copy.wait()


VMEM = pl.BlockSpec(memory_space=pltpu.VMEM)
ANY = pl.BlockSpec(memory_space=pl.ANY)


def body(
    water_content,
    porosity,
    conduct,
    exponent,
    infiltration,
    column_target,
    send_blocks,
    prior_heads,
    block_pattern,
    aquifer_blocks,
    gx_count,
    gy_count,
):
    devices, slots = send_blocks.shape[1:]
    own_blocks, width = prior_heads.shape
    layers, rows, columns = water_content.shape
    most = block_pattern.shape[1]
    hi_rows = -(-(SIDES + 1) * slots // 8) * 8
    part_rows = -(-PARTS * (SIDES + 1) * slots // 16) * 16
    area = own_blocks * width / (rows * columns)
    perms = swaps(gx_count, gy_count)
    in_hbm = lambda array: pltpu.with_memory_space_constraint(array, pltpu.HBM)
    field = jax.ShapeDtypeStruct((own_blocks, width), F32)
    two = jax.ShapeDtypeStruct((2 * own_blocks, width), F32)

    def trade(array):
        return [lax.ppermute(array, BOTH, perm) for perm in perms]

    chunks = rows // 16
    outs = pl.pallas_call(
        functools.partial(soil_kernel, gx_count, gy_count),
        in_specs=[ANY] * 10,
        out_specs=[ANY] + [VMEM] * (SIDES + 4) + [ANY],
        out_shape=[
            jax.ShapeDtypeStruct(water_content.shape, F32),
            jax.ShapeDtypeStruct((2 * most, own_blocks, width), jnp.int32),
            jax.ShapeDtypeStruct((SIDES + 1, own_blocks, width), jnp.int32),
            jax.ShapeDtypeStruct((hi_rows, width), jnp.int32),
        ]
        + [two] * (SIDES + 1)
        + [pltpu.VMEM(aquifer_blocks.shape, F32)],
        scratch_shapes=[
            pltpu.VMEM(water_content.shape, F32),
            *[pltpu.VMEM((rows, columns), F32)] * 4,
            pltpu.VMEM((rows, columns), jnp.int32),
            pltpu.VMEM((own_blocks, width), F32),
            pltpu.VMEM((slots, devices), jnp.int32),
            pltpu.VMEM((own_blocks, most), jnp.int32),
            pltpu.VMEM((rows + 16, columns), F32),
            pltpu.VMEM((2 * part_rows, width // PARTS), F32),
            pltpu.SemaphoreType.DMA((3,)),
            pltpu.SemaphoreType.DMA((chunks, 6)),
            pltpu.SemaphoreType.DMA((chunks,)),
            pltpu.SemaphoreType.DMA,
        ],
        compiler_params=pltpu.CompilerParams(vmem_limit_bytes=24 * 2**20),
        name="soil",
    )(
        *map(
            in_hbm,
            (
                water_content, porosity, conduct, exponent, infiltration, column_target, prior_heads,
                send_blocks[0].T, block_pattern, aquifer_blocks,
            ),
        )
    )
    soil_water, source, block, key, own = outs[:5]
    blocks = pltpu.with_memory_space_constraint(outs[-1], pltpu.VMEM)
    got = [lax.ppermute(out, BOTH, perm) for out, perm in zip(outs[5:], perms)]

    def small(kernel, args, shape, name):
        return pl.pallas_call(
            kernel,
            in_specs=[VMEM] * (2 + len(args)),
            out_specs=VMEM,
            out_shape=shape,
            compiler_params=pltpu.CompilerParams(vmem_limit_bytes=16 * 2**20),
            name=name,
        )(source, blocks, *args)

    r = small(functools.partial(start_kernel, area), (own, *got), field, "start")
    r_sides = trade(r)
    w = small(apply_kernel, (r, *r_sides[::-1]), field, "once")
    w_sides = trade(w)
    v = small(apply_kernel, (w, *w_sides[::-1]), field, "twice")
    v_sides = trade(v)
    sums = small(last_kernel, (r, w, v, *v_sides[::-1]), jax.ShapeDtypeStruct((devices, 1, width), F32), "sums")
    all_sums = lax.all_to_all(sums, BOTH, 0, 0)
    sides = []
    for k in range(SIDES):
        sides += [got[k], r_sides[k], w_sides[k], v_sides[k]]
    heads, column_heads = pl.pallas_call(
        functools.partial(heads_kernel, slots),
        in_specs=[VMEM] * (8 + 4 * SIDES),
        out_specs=[ANY, ANY],
        out_shape=[field, jax.ShapeDtypeStruct((rows, columns), F32)],
        scratch_shapes=[
            pltpu.VMEM((hi_rows, 8, width), F32),
            pltpu.VMEM((own_blocks, width), F32),
            pltpu.VMEM((rows, columns), F32),
            pltpu.SemaphoreType.DMA((1 + rows // 16,)),
        ],
        compiler_params=pltpu.CompilerParams(vmem_limit_bytes=16 * 2**20),
        name="heads",
    )(block, key, all_sums, column_target, own, r, w, v, *sides)
    return soil_water, heads, column_heads


def solution(mesh):
    placed = (
        P(None, "gx", "gy"),
        P("gx", "gy"),
        P("gx", "gy"),
        P("gx", "gy"),
        P("gx", "gy"),
        P("gx", "gy"),
        P(("gx", "gy"), None, None),
        P(("gx", "gy"), None),
        P(("gx", "gy"), None),
        P(("gx", "gy"), None, None, None),
    )
    return jax.shard_map(
        functools.partial(body, gx_count=mesh.shape["gx"], gy_count=mesh.shape["gy"]),
        mesh=mesh,
        in_specs=placed,
        out_specs=(P(None, "gx", "gy"), P(("gx", "gy"), None), P("gx", "gy")),
        check_vma=False,
    )
```
